128 devices in a mesh: col: 32 (over x, y, core), row: 4 (over z).
Axes of the slice: x: 4, y: 4, z: 4, core: 2. Of those that a mesh axis runs over, the one named last changes fastest.
Arguments:
- rhs: float32 [2, 32, 4, 4096], P(None, None, 'row', 'col'), may hold values from -6 to 6
- u_factor: bfloat16 [64, 160, 2, 256, 128], P('row', 'col'), may hold values from -0.0390625 to 0.0390625
- v_factor: bfloat16 [64, 160, 2, 256, 128], P('row', 'col'), may hold values from -0.375 to 0.375
- ranks: int32 [64, 160], P('row', 'col'), may hold values from 8 to 128, as said below
- assign: int32 [160], replicated, may hold values from 0 to 159, each once
Outputs:
- solution: float32 [2, 32, 40960], P(None, None, 'col')
- residual_estimate: float32 [32], replicated
The draws below stay inside these ranges and needn't reach their ends.
Inputs may be any that keep to these rules, and one draw needn't show every extreme that they name: `ranks`: every entry is 128 // 16 times a power of two from 1 to 16.
All inputs are finite; a program needn't handle non-finite values.
Results may differ from the reference program's by a relative error of at most 0.0068.
Values may be sent and summed in bfloat16 or wider, within the bound.
A program may use at most 128 MiB of HBM per device.

```python
import jax
import jax.numpy as jnp
from jax import lax

NB = 256
RMAX = 128
NS = 32
ITERS = 2
TR = 64
TC = 160
MR = 4096
N_ROW = 4


def draw_ranks(key, part):
    first = jax.random.randint(jax.random.fold_in(key, 11), (TR, TC), 0, 5)
    second = jax.random.randint(jax.random.fold_in(key, 12), (TR, TC), 0, 5)
    level = jnp.minimum(first, second)
    values = RMAX // 16 * jnp.left_shift(jnp.ones_like(level), level)
    values = values.at[0, 0].set(RMAX).at[0, 1].set(RMAX // 16)
    return values.astype(jnp.int32)


def level_of(rng, shape, cuts, smallest, high):
    factor_of = 1.0
    for position, shards_of in cuts:
        draws = jax.random.uniform(jax.random.fold_in(jax.random.fold_in(rng, 6), position), (shards_of,), jnp.float32, smallest / len(cuts), high / len(cuts))
        factor_of = factor_of * jnp.repeat(jnp.exp(draws), shape[position] // shards_of).reshape((-1,) + (1,) * (len(shape) - 1 - position))
    return factor_of


def noise(own_key, shape, spread, limit, split=(), kind=jnp.bfloat16):
    level = level_of(own_key, shape, split, -0.22, 0.18) if split else 1.0
    array = jax.random.normal(own_key, shape, jnp.float32) * spread * level
    return jnp.minimum(jnp.maximum(array, -limit), limit).astype(kind)


def setup_inputs(seed: int = 0) -> dict:
    key_of = jax.random.split(jax.random.key(seed), 6)
    return {
        "rhs": noise(key_of[0], (2, NS, N_ROW, MR), 1.0, 6.0, ((2, 4), (3, 32)), jnp.float32),
        "u_factor": noise(key_of[1], (TR, TC, 2, NB, RMAX), (RMAX * TC) ** -0.5, 0.0390625, ((0, 4), (1, 32))),
        "v_factor": noise(key_of[2], (TR, TC, 2, NB, RMAX), NB ** -0.5, 0.375, ((0, 4), (1, 32))),
        "ranks": draw_ranks(jax.random.fold_in(key_of[5], 71), 0),
        "assign": jax.random.permutation(key_of[4], TC).astype(jnp.int32),
    }


HIGH = lax.Precision.HIGHEST

def rounded(value):
    return lax.optimization_barrier(value.astype(jnp.bfloat16)).astype(jnp.float32)

def sum_squares(value):
    return lax.optimization_barrier(jnp.sum(value * value, axis=(0, 2)))

def reference(rhs, u_factor, v_factor, ranks, assign):
    tile_rows, tile_cols = ranks.shape
    tile_size = u_factor.shape[3]
    rank_cap = u_factor.shape[4]
    sources = rhs.shape[1]
    rank_iota = lax.broadcasted_iota(jnp.int32, (tile_rows, tile_cols, 1, 1, rank_cap), 4)
    mask = (rank_iota < ranks[:, :, None, None, None]).astype(jnp.float32)

    def forward(model_vec):
        model_b = rounded(model_vec).reshape(2, sources, tile_cols, tile_size)

        def one_row(packed):
            left, right, mask_row = packed
            raw = jnp.einsum('pcnk,dspn->pcdsk', right.astype(jnp.float32), model_b, precision=HIGH)
            coeff = jnp.stack([raw[:, 0, 0] - raw[:, 1, 1], raw[:, 0, 1] + raw[:, 1, 0]], axis=1) * mask_row
            coeff = rounded(coeff)
            prod = jnp.einsum('pcnk,pdsk->cdsn', left.astype(jnp.float32), coeff, precision=HIGH)
            return jnp.stack([prod[0, 0] - prod[1, 1], prod[0, 1] + prod[1, 0]], axis=0)
        blocks = lax.map(one_row, (u_factor, v_factor, mask))
        return jnp.transpose(blocks, (1, 2, 0, 3)).reshape(2, sources, tile_rows * tile_size)

    def adjoint(data_vec):
        data_b = rounded(data_vec).reshape(2, sources, tile_rows, tile_size)
        data_b = jnp.transpose(data_b, (2, 0, 1, 3))

        def one_row(carry, packed):
            left, right, mask_row, data_row = packed
            raw = jnp.einsum('pcnk,dsn->pcdsk', left.astype(jnp.float32), data_row, precision=HIGH)
            coeff = jnp.stack([raw[:, 0, 0] + raw[:, 1, 1], raw[:, 0, 1] - raw[:, 1, 0]], axis=1) * mask_row
            coeff = rounded(coeff)
            prod = jnp.einsum('pcnk,pdsk->cdspn', right.astype(jnp.float32), coeff, precision=HIGH)
            part = jnp.stack([prod[0, 0] + prod[1, 1], prod[0, 1] - prod[1, 0]], axis=0)
            return (carry + part, None)
        start = jnp.zeros((2, sources, tile_cols, tile_size), jnp.float32)
        total, _ = lax.scan(one_row, start, (u_factor, v_factor, mask, data_b))
        return total.reshape(2, sources, tile_cols * tile_size)
    data_hat = rhs.reshape(2, sources, tile_rows * tile_size)
    beta_now = jnp.sqrt(sum_squares(data_hat))
    u_vec = data_hat / beta_now[None, :, None]
    v_hat = adjoint(data_hat) / beta_now[None, :, None]
    alpha_now = jnp.sqrt(sum_squares(v_hat))
    v_vec = v_hat / alpha_now[None, :, None]
    w_vec = v_vec
    x_vec = jnp.zeros_like(v_vec)
    phibar = beta_now
    rhobar = alpha_now
    for iteration in range(ITERS):
        data_hat = forward(v_vec) - alpha_now[None, :, None] * u_vec
        beta_now = jnp.sqrt(sum_squares(data_hat))
        u_vec = data_hat / beta_now[None, :, None]
        v_hat = adjoint(data_hat) / beta_now[None, :, None] - beta_now[None, :, None] * v_vec
        alpha_now = jnp.sqrt(sum_squares(v_hat))
        v_vec = v_hat / alpha_now[None, :, None]
        rho_now = jnp.sqrt(rhobar * rhobar + beta_now * beta_now)
        cosine = rhobar / rho_now
        sine = beta_now / rho_now
        theta = sine * alpha_now
        rhobar = -cosine * alpha_now
        phi_now = cosine * phibar
        phibar = sine * phibar
        x_vec = x_vec + (phi_now / rho_now)[None, :, None] * w_vec
        w_vec = v_vec - (theta / rho_now)[None, :, None] * w_vec
    inverse = jnp.zeros((tile_cols,), jnp.int32).at[assign].set(jnp.arange(tile_cols, dtype=jnp.int32))
    natural = x_vec.reshape(2, sources, tile_cols, tile_size)[:, :, inverse]
    return (natural.reshape(2, sources, tile_cols * tile_size), phibar)
```

```python
import jax
import jax.numpy as jnp
from jax import lax
from jax.sharding import Mesh
from jax.sharding import PartitionSpec as P

ITERS = 2
COL = ("col_0", "col_1", "col_2")
COL_ROW = ("col_0", "col_1", "col_2", "row")


def cut_along(x, dim, devices):
    before, after = (x.shape[:dim], x.shape[dim + 1 :])
    return jnp.moveaxis(x.reshape(*before, devices, -1, *after), dim, 0)


def sent_and_summed(x, axis, dim):
    devices = lax.axis_size(axis)
    tiles = lax.all_to_all(cut_along(x, dim, devices), axis, 0, 0, tiled=True)
    return jnp.sum(tiles.astype(jnp.float32), axis=0)


def in_order(tiles, dim):
    tiles = jnp.moveaxis(tiles, 0, dim)
    dims = tiles.shape
    return tiles.reshape(*dims[:dim], dims[dim] * dims[dim + 1], *dims[dim + 2 :])


def copy_for_each(x, axis):
    copies = jnp.broadcast_to(x, (lax.axis_size(axis), *x.shape))
    return lax.all_to_all(copies, axis, split_axis=0, concat_axis=0, tiled=True)


def collect(x, axis, dim):
    return in_order(copy_for_each(x, axis), dim)


def by_axis(x, axes):
    for axis in axes:
        x = lax.psum(x, axis)
    return x


def over_copies(x, axis):
    everything = copy_for_each(x, axis)
    return jnp.sum(everything.astype(jnp.float32), axis=0)


def over_copies_2(x, axis):
    everything = copy_for_each(x, axis)
    return jnp.sum(everything, axis=0)


def sum_squares(value):
    return jnp.sum(value * value, axis=(0, 2))


def on_device(rhs, u_factor, v_factor, ranks, assign):
    tile_rows = u_factor.shape[0]
    tile_cols = u_factor.shape[1]
    tile_size = u_factor.shape[3]
    rank_cap = u_factor.shape[4]
    sources = rhs.shape[1]
    rank_iota = lax.broadcasted_iota(jnp.int32, (tile_rows, tile_cols, 1, 1, rank_cap), 4)
    mask = (rank_iota < ranks[:, :, None, None, None]).astype(jnp.float32)

    def adjoint_terms(group_data):
        data_b = group_data.reshape(2, sources, tile_rows, tile_size)
        raw = jnp.einsum("ipcnk,dsin->ipcdsk", u_factor, data_b, preferred_element_type=jnp.float32)
        coeff = jnp.stack(
            [raw[:, :, 0, 0] + raw[:, :, 1, 1], raw[:, :, 0, 1] - raw[:, :, 1, 0]], axis=2
        )
        coeff = (coeff * mask).astype(jnp.bfloat16)
        prod = jnp.einsum("ipcnk,ipdsk->cdspn", v_factor, coeff, preferred_element_type=jnp.float32)
        partial_model = jnp.stack([prod[0, 0] + prod[1, 1], prod[0, 1] - prod[1, 0]], axis=0)
        return partial_model.reshape(2, sources, tile_cols * tile_size)

    def adjoint_step(data_hat, v_prev):
        group_data = collect(data_hat.astype(jnp.bfloat16), COL, 2)
        beta_now = jnp.sqrt(by_axis(sum_squares(data_hat), COL_ROW))
        model_sum = over_copies(adjoint_terms(group_data).astype(jnp.bfloat16), "row").astype(
            jnp.float32
        )
        v_hat = model_sum / beta_now[None, :, None] - beta_now[None, :, None] * v_prev
        alpha_now = jnp.sqrt(over_copies_2(sum_squares(v_hat), COL))
        return (
            data_hat / beta_now[None, :, None],
            beta_now,
            v_hat / alpha_now[None, :, None],
            alpha_now,
        )

    data_first = rhs.reshape(2, sources, rhs.shape[3])
    zero_model = jnp.zeros((2, sources, tile_cols * tile_size), jnp.float32)
    u_vec, beta_now, v_vec, alpha_now = adjoint_step(data_first, zero_model)
    w_vec = v_vec
    x_vec = zero_model
    phibar = beta_now
    rhobar = alpha_now
    for iteration in range(ITERS):
        model_b = v_vec.astype(jnp.bfloat16).reshape(2, sources, tile_cols, tile_size)
        forward_raw = jnp.einsum(
            "ipcnk,dspn->ipcdsk", v_factor, model_b, preferred_element_type=jnp.float32
        )
        forward_coeff = jnp.stack(
            [
                forward_raw[:, :, 0, 0] - forward_raw[:, :, 1, 1],
                forward_raw[:, :, 0, 1] + forward_raw[:, :, 1, 0],
            ],
            axis=2,
        )
        forward_coeff = (forward_coeff * mask).astype(jnp.bfloat16)
        forward_prod = jnp.einsum(
            "ipcnk,ipdsk->cdsin", u_factor, forward_coeff, preferred_element_type=jnp.float32
        )
        partial_data = jnp.stack(
            [forward_prod[0, 0] - forward_prod[1, 1], forward_prod[0, 1] + forward_prod[1, 0]],
            axis=0,
        )
        partial_data = partial_data.reshape(2, sources, tile_rows * tile_size)
        data_hat = (
            sent_and_summed(partial_data.astype(jnp.bfloat16), COL, 2)
            - alpha_now[None, :, None] * u_vec
        )
        u_vec, beta_now, v_vec, alpha_now = adjoint_step(data_hat, v_vec)
        rho_now = jnp.sqrt(rhobar * rhobar + beta_now * beta_now)
        cosine = rhobar / rho_now
        sine = beta_now / rho_now
        theta = sine * alpha_now
        rhobar = -cosine * alpha_now
        phi_now = cosine * phibar
        phibar = sine * phibar
        x_vec = x_vec + (phi_now / rho_now)[None, :, None] * w_vec
        w_vec = v_vec - (theta / rho_now)[None, :, None] * w_vec
    all_cols = assign.shape[0]
    natural = lax.axis_index(COL) * tile_cols + jnp.arange(tile_cols, dtype=jnp.int32)
    positions = jnp.arange(all_cols, dtype=jnp.int32)
    where_held = jnp.sum(
        positions[None, :] * (assign[None, :] == natural[:, None]).astype(jnp.int32), axis=1
    )
    share = sources // lax.axis_size("row")
    own_share = lax.dynamic_slice_in_dim(x_vec, lax.axis_index("row") * share, share, 1)
    gathered = collect(own_share, COL, 2)
    gathered = gathered.reshape(2, share, all_cols, tile_size)
    picked = jnp.concatenate(
        [lax.dynamic_slice_in_dim(gathered, where_held[j], 1, axis=2) for j in range(tile_cols)],
        axis=2,
    ).reshape(2, share, tile_cols * tile_size)
    solution = collect(picked, "row", 1)
    return (solution, phibar)


def solution(mesh):
    split = Mesh(
        mesh.devices.reshape(4, 4, 2, mesh.shape["row"]), ("col_0", "col_1", "col_2", "row")
    )
    placed = (
        P(None, None, "row", COL),
        P("row", COL, None, None, None),
        P("row", COL, None, None, None),
        P("row", COL),
        P(),
    )
    return jax.shard_map(
        on_device, mesh=split, in_specs=placed, out_specs=(P(None, None, COL), P()), check_vma=False
    )
```

```python
import functools
import math

import jax
import jax.numpy as jnp
from jax import lax
from jax.experimental import pallas as pl
from jax.experimental.pallas import tpu as pltpu
from jax.sharding import PartitionSpec as P

F32 = jnp.float32
BF16 = jnp.bfloat16
MESH = pl.DeviceIdType.MESH
LANES = 128
GROUP = 2


def nn(lhs, rhs):
    return jnp.dot(lhs, rhs, preferred_element_type=F32)


def nt(lhs, rhs):
    return lax.dot_general(lhs, rhs, (((1,), (1,)), ((), ())), preferred_element_type=F32)


def lanes(*parts):
    return jnp.concatenate(parts, axis=1)


def stacked(*parts):
    return jnp.concatenate(parts, axis=0)


def times_factor(vec):
    half = vec.shape[0] // 2
    re, im = vec[:half], vec[half:]
    return stacked(lanes(re, -im), lanes(im, re))


def times_conj_factor(vec):
    half = vec.shape[0] // 2
    re, im = vec[:half], vec[half:]
    return stacked(lanes(re, im), lanes(im, -re))


def to_row(acc):
    pad = jnp.zeros((LANES - acc.shape[0], LANES), F32)
    return jnp.sum(stacked(acc, pad).T, axis=0, keepdims=True)


def to_col(row, sources):
    col = jnp.broadcast_to(row, (LANES, LANES)).T[:sources]
    return stacked(col, col)


def kernel(
    dims,
    rhs,
    u_hbm,
    v_hbm,
    ranks,
    assign,
    out,
    phi_out,
    d_out,
    v_own,
    u_fac,
    v_fac,
    d_full,
    y_send,
    y_recv,
    z_acc,
    z_send,
    z_recv,
    v_full,
    lhs_p,
    gathered0,
    gathered1,
    picked,
    sib_recv,
    natural,
    cols,
    row_send,
    row_recv,
    zrow_send,
    zrow_recv,
    fac_sem,
    ag_s,
    ag_r,
    ys_s,
    ys_r,
    row_s,
    row_r,
    zr_s,
    zr_r,
    zs_s,
    zs_r,
    zg_s,
    zg_r,
    ng_s,
    ng_r,
    sib_s,
    sib_r,
    nz_s,
    nz_r,
):
    chips, nx, ny, nz, tile_cols, sources = dims
    rows = 2 * sources
    zrows = rows // nz
    gathered = (gathered0, gathered1)
    me_c, me_z = lax.axis_index("col"), lax.axis_index("row")
    chip, core = lax.div(me_c, 2), lax.rem(me_c, 2)
    cx, cy = lax.div(chip, ny), lax.rem(chip, ny)

    def chip_to(q):
        return lax.rem(cx + lax.div(q, ny), nx) * ny + lax.rem(cy + lax.rem(q, ny), ny)

    def chip_from(q):
        return lax.rem(cx + nx - lax.div(q, ny), nx) * ny + lax.rem(cy + ny - lax.rem(q, ny), ny)

    def remote(src, dst, send, recv, col, row):
        return pltpu.make_async_remote_copy(
            src_ref=src, dst_ref=dst, send_sem=send, recv_sem=recv,
            device_id=(col, row), device_id_type=MESH,
        )

    def in_plane(k):
        return chip_to(lax.div(k, 2)) * 2 + lax.rem(core + lax.rem(k, 2), 2)

    def along_z(k):
        return lax.rem(me_z + k, nz)

    def copy_ag(rd, k):
        own = d_full.at[rd, chip, core]
        return remote(own, own, ag_s.at[rd, k], ag_r.at[rd, k], in_plane(k), me_z)

    def copy_ys(rd, k):
        to_chip, to_core = chip_to(lax.div(k, 2)), lax.rem(core + lax.rem(k, 2), 2)
        return remote(
            y_send.at[rd, to_chip, to_core], y_recv.at[rd, k], ys_s.at[rd, k], ys_r.at[rd, k],
            to_chip * 2 + to_core, me_z,
        )

    def copy_row(rd, k):
        return remote(
            row_send.at[rd], row_recv.at[rd, k], row_s.at[rd, k], row_r.at[rd, k], in_plane(k), me_z
        )

    def copy_zrow(rd, k):
        return remote(
            zrow_send.at[rd], zrow_recv.at[rd, k], zr_s.at[rd, k], zr_r.at[rd, k], me_c, along_z(k)
        )

    def copy_zs(rd, k):
        return remote(
            z_send.at[rd, along_z(k)], z_recv.at[rd, k], zs_s.at[rd, k], zs_r.at[rd, k], me_c,
            along_z(k),
        )

    def copy_zg(rd, k):
        own = v_full.at[rd, me_z]
        return remote(own, own, zg_s.at[rd, k], zg_r.at[rd, k], me_c, along_z(k))

    def copy_ng(rd, q):
        own = gathered[rd].at[pl.ds(chip * tile_cols, tile_cols)]
        return remote(own, own, ng_s.at[rd, q], ng_r.at[rd, q], chip_to(q) * 2 + core, me_z)

    def copy_sib(rd):
        return remote(
            picked.at[rd, 1 - core], sib_recv.at[rd], sib_s.at[rd], sib_r.at[rd],
            chip * 2 + 1 - core, me_z,
        )

    def copy_nz(rd, k):
        own = natural.at[rd, me_z]
        return remote(own, own, nz_s.at[rd, k], nz_r.at[rd, k], me_c, along_z(k))

    def loop(low, high, body):
        lax.fori_loop(low, high, lambda i, c: (body(i), c)[1], 0)

    def factor_copies(i):
        return (
            pltpu.make_async_copy(u_hbm.at[i], u_fac.at[i], fac_sem.at[0, i]),
            pltpu.make_async_copy(v_hbm.at[i], v_fac.at[i], fac_sem.at[1, i]),
        )

    lane = lax.broadcasted_iota(jnp.int32, (rows, LANES), 1)

    def masked(value, i, p):
        return jnp.where(lane < ranks[i, p], value, 0.0).astype(BF16)

    def lane_sums(square, acc):
        for at in range(0, square.shape[1], LANES):
            part = square[:, at : at + LANES]
            acc = acc + part[:sources] + part[sources:]
        return acc

    def start_factor(q):
        for copy in factor_copies(chip_from(q)):
            copy.start()

    loop(0, chips, start_factor)
    d_full[0, chip, core] = rhs[...].astype(BF16)

    barrier = pltpu.get_barrier_semaphore()

    def greet(k):
        pl.semaphore_signal(barrier, inc=1, device_id=(in_plane(k), me_z), device_id_type=MESH)

    def greet_z(k):
        pl.semaphore_signal(barrier, inc=1, device_id=(me_c, along_z(k)), device_id_type=MESH)

    loop(1, 2 * chips, greet)
    loop(1, nz, greet_z)
    pl.semaphore_wait(barrier, 2 * chips - 1 + nz - 1)
    loop(1, 2 * chips, lambda k: copy_ag(0, k).start())

    def adjoint(rd):
        z_acc[...] = jnp.zeros_like(z_acc)

        def group(g, acc):
            parts = [[] for _ in range(tile_cols)]
            where = []
            for j in range(GROUP):
                q = g * GROUP + j
                i = chip_from(q)
                where.append(i)

                @pl.when(q > 0)
                def _():
                    copy_ag(rd, 2 * q).wait_recv()

                copy_ag(rd, 2 * q + 1).wait_recv()
                if rd == 0:
                    for copy in factor_copies(i):
                        copy.wait()
                data = lanes(d_full[rd, i, 0], d_full[rd, i, 1])
                wide = data.astype(F32)
                acc = lane_sums(wide * wide, acc)
                left = times_conj_factor(data)
                right = lanes(*[u_fac[i, p].reshape(-1, LANES) for p in range(tile_cols)])
                raw = nn(left, right)
                for p in range(tile_cols):
                    coeff = masked(raw[:, p * LANES : (p + 1) * LANES], i, p)
                    parts[p].append(times_conj_factor(coeff))
            for p in range(tile_cols):
                right = lanes(*[v_fac[i, p, c] for i in where for c in range(2)])
                z_acc[p] += nt(lanes(*parts[p]), right)
            return acc

        return lax.fori_loop(0, chips // GROUP, group, jnp.zeros((sources, LANES), F32))

    def start_model(rd):
        for r in range(nz):
            z_send[rd, r] = z_acc[:, r * zrows : (r + 1) * zrows, :].astype(BF16)
        loop(1, nz, lambda k: copy_zs(rd, k).start())

    def zrow_start(rd, row):
        zrow_send[rd] = row
        loop(1, nz, lambda k: copy_zrow(rd, k).start())

    def zrow_sum(rd):
        total = zrow_send[rd]
        for k in range(1, nz):
            copy_zrow(rd, k).wait_recv()
            total = total + zrow_recv[rd, k]
        return total

    own_rows = pl.ds(pl.multiple_of(me_z * zrows, zrows), zrows)

    def own_col(slot):
        part = cols[slot, own_rows, :]
        return lanes(part, part)[None]

    def model_sum(rd):
        total = z_acc[:, own_rows, :]
        for k in range(1, nz):
            copy_zs(rd, k).wait_recv()
            total = total + z_recv[rd, k].astype(F32)
        return total

    def send_model(rd, v_hat):
        v_own[rd] = v_hat
        v_b = v_hat.astype(BF16)
        v_full[rd, me_z] = v_b
        loop(1, nz, lambda k: copy_zg(rd, k).start())
        gathered[rd][pl.ds(chip * tile_cols, tile_cols)] = v_b
        loop(1, chips, lambda q: copy_ng(rd, q).start())

    def forward(rd):
        for k in range(1, nz):
            copy_zg(rd, k).wait_recv()
        acc = jnp.zeros((sources, LANES), F32)
        for p in range(tile_cols):
            vec = stacked(*[v_full[rd, r, p] for r in range(nz)])
            wide = vec.astype(F32)
            acc = lane_sums(wide * wide, acc)
            lhs_p[p] = times_factor(vec)
        row_send[rd] = to_row(acc)
        loop(1, 2 * chips, lambda k: copy_row(rd, k).start())

        def group(g):
            qs = [chips - 1 - (g * GROUP + j) for j in range(GROUP)]
            where = [chip_to(q) for q in qs]
            parts = [[] for _ in range(GROUP)]
            for p in range(tile_cols):
                right = lanes(*[v_fac[i, p].reshape(-1, LANES) for i in where])
                raw = nn(lhs_p[p], right)
                for j, i in enumerate(where):
                    coeff = masked(raw[:, j * LANES : (j + 1) * LANES], i, p)
                    parts[j].append(times_factor(coeff))
            for j, i in enumerate(where):
                right = lanes(*[u_fac[i, p, c] for p in range(tile_cols) for c in range(2)])
                y = nt(lanes(*parts[j]), right).astype(BF16)
                y_send[rd, i, 0] = y[:, :LANES]
                y_send[rd, i, 1] = y[:, LANES:]

                @pl.when(qs[j] > 0)
                def _():
                    copy_ys(rd, 2 * qs[j]).start()

                copy_ys(rd, 2 * qs[j] + 1).start()

        loop(0, chips // GROUP, group)

    def row_sum(rd):
        def add(k, total):
            copy_row(rd, k).wait_recv()
            return total + row_recv[rd, k]

        return lax.fori_loop(1, 2 * chips, add, row_send[rd])

    def data_sum(rd):
        def add(k, total):
            copy_ys(rd, k).wait_recv()
            return total + y_recv[rd, k].astype(F32)

        return lax.fori_loop(1, 2 * chips, add, y_send[rd, chip, core].astype(F32))

    def pick(rd, held):
        for q in range(1, chips):
            copy_ng(rd, q).wait_recv()
        for j, (found, at) in enumerate(held):
            seg = gathered[rd][at].astype(F32) * found.astype(F32)
            picked[rd, j // tile_cols, j % tile_cols] = seg.astype(BF16)
        copy_sib(rd).start()

    def join(rd):
        copy_sib(rd).wait_recv()
        mine = picked[rd, core].astype(F32) + sib_recv[rd].astype(F32)
        natural[rd, me_z] = mine.astype(BF16)
        loop(1, nz, lambda k: copy_nz(rd, k).start())

    def find_held():
        first = chip * (2 * tile_cols)
        zero = jnp.int32(0)

        def step(a, carry):
            found, at = list(carry[0]), list(carry[1])
            for t in range(tile_cols):
                held = assign[a * (2 * tile_cols) + core * tile_cols + t] - first
                for j in range(2 * tile_cols):
                    hit = held == j
                    found[j] = jnp.where(hit, 1, found[j])
                    at[j] = jnp.where(hit, a * tile_cols + t, at[j])
            return tuple(found), tuple(at)

        many = 2 * tile_cols
        found, at = lax.fori_loop(0, chips, step, ((zero,) * many, (zero,) * many))
        return list(zip(found, at))

    acc = adjoint(0)
    start_model(0)
    zrow_start(0, to_row(acc))
    beta0 = jnp.sqrt(zrow_sum(0))
    cols[0] = to_col(beta0, sources)
    v_hat = model_sum(0) / own_col(0)
    send_model(0, v_hat)

    forward(0)
    held = find_held()
    alpha0 = jnp.sqrt(row_sum(0))
    cols[1] = to_col(alpha0, sources)
    d_hat = data_sum(0) / cols[1] - cols[1] * (rhs[...] / cols[0])
    d_full[1, chip, core] = d_hat.astype(BF16)
    loop(1, 2 * chips, lambda k: copy_ag(1, k).start())
    d_out[...] = d_hat
    pick(0, held)
    acc = adjoint(1)
    start_model(1)
    zrow_start(1, to_row(acc))
    join(0)
    beta1 = jnp.sqrt(zrow_sum(1))
    cols[2] = to_col(beta1, sources)
    v_hat = model_sum(1) / own_col(2) - own_col(2) * (v_own[0] / own_col(1))
    send_model(1, v_hat)

    forward(1)
    alpha1 = jnp.sqrt(row_sum(1))
    cols[3] = to_col(alpha1, sources)
    d_hat = data_sum(1) / cols[3] - cols[3] * (d_out[...] / cols[2])
    square = d_hat * d_hat
    row_send[2] = to_row(square[:sources] + square[sources:])
    loop(1, 2 * chips, lambda k: copy_row(2, k).start())
    d_out[...] = d_hat
    pick(1, held)
    zrow_start(2, row_sum(2))
    join(1)
    rho1 = jnp.sqrt(alpha0 * alpha0 + beta1 * beta1)
    cosine = alpha0 / rho1
    sine = beta1 / rho1
    theta = sine * alpha1
    rhobar = -cosine * alpha1
    phi1 = cosine * beta0
    phibar = sine * beta0
    beta2 = jnp.sqrt(zrow_sum(2))
    rho2 = jnp.sqrt(rhobar * rhobar + beta2 * beta2)
    cosine = rhobar / rho2
    sine = beta2 / rho2
    step2 = cosine * phibar / rho2
    phi_out[0:1] = sine * phibar
    phi_out[1:2] = sine / rho2
    phi_out[2:3] = theta / rho1
    phi_out[3:4] = alpha0
    phi_out[4:5] = alpha1
    first = to_col((phi1 / rho1 - step2 * (theta / rho1)) / alpha0, sources)
    second = to_col(step2 / alpha1, sources)
    for rd in range(2):
        for k in range(1, nz):
            copy_nz(rd, k).wait_recv()
    width = natural.shape[-1]
    for p in range(tile_cols):
        for at in range(0, width, LANES):
            one = stacked(*[natural[0, r, p, :, at : at + LANES] for r in range(nz)])
            two = stacked(*[natural[1, r, p, :, at : at + LANES] for r in range(nz)])
            out[:, p * width + at : p * width + at + LANES] = (
                first * one.astype(F32) + second * two.astype(F32)
            )

    for rd in range(2):
        loop(1, 2 * chips, lambda k, rd=rd: copy_ag(rd, k).wait_send())
        loop(1, 2 * chips, lambda k, rd=rd: copy_ys(rd, k).wait_send())
        loop(1, nz, lambda k, rd=rd: copy_zs(rd, k).wait_send())
        loop(1, nz, lambda k, rd=rd: copy_zg(rd, k).wait_send())
        loop(1, nz, lambda k, rd=rd: copy_nz(rd, k).wait_send())
        loop(1, chips, lambda k, rd=rd: copy_ng(rd, k).wait_send())
        copy_sib(rd).wait_send()
    for rd in range(3):
        loop(1, 2 * chips, lambda k, rd=rd: copy_row(rd, k).wait_send())
        loop(1, nz, lambda k, rd=rd: copy_zrow(rd, k).wait_send())


def last_adjoint(d_hat, v_hats, scalars, u_factor, v_factor, ranks):
    tile_rows, tile_cols, _, tile_size, rank_cap = u_factor.shape
    sources = d_hat.shape[0] // 2
    rank_iota = lax.broadcasted_iota(jnp.int32, (tile_rows, tile_cols, 1, 1, rank_cap), 4)
    mask = (rank_iota < ranks[:, :, None, None, None]).astype(F32)
    d_hat = d_hat.reshape(2, sources, -1)
    beta = jnp.sqrt(lax.psum(jnp.sum(d_hat * d_hat, axis=(0, 2)), ("col", "row")))
    data = lax.all_gather(d_hat.astype(BF16), "col", axis=2, tiled=True)
    data = data.reshape(2, sources, tile_rows, tile_size)
    raw = jnp.einsum("ipcnk,dsin->ipcdsk", u_factor, data, preferred_element_type=F32)
    coeff = jnp.stack([raw[:, :, 0, 0] + raw[:, :, 1, 1], raw[:, :, 0, 1] - raw[:, :, 1, 0]], axis=2)
    coeff = (coeff * mask).astype(BF16)
    prod = jnp.einsum("ipcnk,ipdsk->cdspn", v_factor, coeff, preferred_element_type=F32)
    model = jnp.stack([prod[0, 0] + prod[1, 1], prod[0, 1] - prod[1, 0]], axis=0)
    model = lax.psum(model, "row").reshape(2, sources, tile_cols * tile_size)
    sine_by_rho, theta_by_rho, alpha0, alpha1 = [row[None, :, None] for row in scalars]
    v_hats = lax.all_gather(v_hats, "row", axis=2, tiled=True)
    v_hats = v_hats.transpose(0, 2, 1, 3).reshape(2, *model.shape)
    v_prev = v_hats[1] / alpha1
    w_prev = v_prev - theta_by_rho * (v_hats[0] / alpha0)
    v_hat = model / beta[None, :, None] - beta[None, :, None] * v_prev
    alpha = jnp.sqrt(lax.psum(jnp.sum(v_hat * v_hat, axis=(0, 2)), "col"))
    v_vec = v_hat / alpha[None, :, None]
    return v_vec, alpha, v_vec - sine_by_rho * alpha[None, :, None] * w_prev


def on_device(nz, rhs, u_factor, v_factor, ranks, assign):
    tile_rows, tile_cols, _, tile_size, _ = u_factor.shape
    sources = rhs.shape[1]
    rows = 2 * sources
    zrows = rows // nz
    chips = tile_rows
    ny = math.isqrt(chips)
    nx = chips // ny
    dims = (chips, nx, ny, nz, tile_cols, sources)
    seg = (tile_cols, zrows, tile_size)
    dma = pltpu.SemaphoreType.DMA
    vmem = pl.BlockSpec(memory_space=pltpu.VMEM)
    smem = pl.BlockSpec(memory_space=pltpu.SMEM)
    hbm = pl.BlockSpec(memory_space=pl.ANY)
    peers, zs = (2, 2 * chips), (2, nz)
    out, scalars, d_hat, v_hats = pl.pallas_call(
        functools.partial(kernel, dims),
        out_shape=[
            jax.ShapeDtypeStruct((rows, tile_cols * tile_size), F32),
            jax.ShapeDtypeStruct((5, LANES), F32),
            jax.ShapeDtypeStruct((rows, LANES), F32),
            jax.ShapeDtypeStruct((2, *seg), F32),
        ],
        in_specs=[vmem, hbm, hbm, smem, smem],
        out_specs=[vmem] * 4,
        scratch_shapes=[
            pltpu.VMEM(u_factor.shape, BF16),
            pltpu.VMEM(v_factor.shape, BF16),
            pltpu.VMEM((2, chips, 2, rows, LANES), BF16),
            pltpu.VMEM((2, chips, 2, rows, LANES), BF16),
            pltpu.VMEM((2, 2 * chips, rows, LANES), BF16),
            pltpu.VMEM((tile_cols, rows, tile_size), F32),
            pltpu.VMEM((2, nz, *seg), BF16),
            pltpu.VMEM((2, nz, *seg), BF16),
            pltpu.VMEM((2, nz, *seg), BF16),
            pltpu.VMEM((tile_cols, rows, 2 * tile_size), BF16),
            pltpu.VMEM((chips * tile_cols, zrows, tile_size), BF16),
            pltpu.VMEM((chips * tile_cols, zrows, tile_size), BF16),
            pltpu.VMEM((2, 2, *seg), BF16),
            pltpu.VMEM((2, *seg), BF16),
            pltpu.VMEM((2, nz, *seg), BF16),
            pltpu.VMEM((4, rows, LANES), F32),
            pltpu.VMEM((3, 1, LANES), F32),
            pltpu.VMEM((3, 2 * chips, 1, LANES), F32),
            pltpu.VMEM((3, 1, LANES), F32),
            pltpu.VMEM((3, nz, 1, LANES), F32),
            dma((2, chips)),
            dma(peers), dma(peers),
            dma(peers), dma(peers),
            dma((3, 2 * chips)), dma((3, 2 * chips)),
            dma((3, nz)), dma((3, nz)),
            dma(zs), dma(zs),
            dma(zs), dma(zs),
            dma((2, chips)), dma((2, chips)),
            dma((2,)), dma((2,)),
            dma(zs), dma(zs),
        ],
        compiler_params=pltpu.CompilerParams(
            collective_id=0, has_side_effects=True, vmem_limit_bytes=58 * 2**20
        ),
        name="lsqr",
    )(rhs.reshape(rows, LANES), u_factor, v_factor, ranks, assign)
    last_adjoint(d_hat, v_hats, scalars[1:, :sources], u_factor, v_factor, ranks)
    phibar = scalars[0, :sources]
    return out.reshape(2, sources, tile_cols * tile_size), phibar


def solution(mesh):
    return jax.shard_map(
        functools.partial(on_device, mesh.shape["row"]),
        mesh=mesh,
        in_specs=(
            P(None, None, "row", "col"),
            P("row", "col", None, None, None),
            P("row", "col", None, None, None),
            P("row", "col"),
            P(),
        ),
        out_specs=(P(None, None, "col"), P()),
        check_vma=False,
    )
```

```python
import functools
import math

import jax
import jax.numpy as jnp
from jax import lax
from jax.experimental import pallas as pl
from jax.experimental.pallas import tpu as pltpu
from jax.sharding import PartitionSpec as P

F32 = jnp.float32
BF16 = jnp.bfloat16
MESH = pl.DeviceIdType.MESH
LANES = 128
GROUP = 4
LOAD = 2
AHEAD = 2
UNROLL = 16
BEHIND = 1


def nn(lhs, rhs):
    return jnp.dot(lhs, rhs, preferred_element_type=F32)


def nt(lhs, rhs):
    return lax.dot_general(lhs, rhs, (((1,), (1,)), ((), ())), preferred_element_type=F32)


def lanes(*parts):
    return jnp.concatenate(parts, axis=1)


def stacked(*parts):
    return jnp.concatenate(parts, axis=0)


def times_factor(vec):
    half = vec.shape[0] // 2
    re, im = vec[:half], vec[half:]
    return stacked(lanes(re, -im), lanes(im, re))


def times_conj_factor(vec):
    half = vec.shape[0] // 2
    re, im = vec[:half], vec[half:]
    return stacked(lanes(re, im), lanes(im, -re))


def to_row(acc):
    pad = jnp.zeros((LANES - acc.shape[0], LANES), F32)
    return jnp.sum(stacked(acc, pad).T, axis=0, keepdims=True)


def to_col(row, sources):
    col = jnp.broadcast_to(row, (LANES, LANES)).T[:sources]
    return stacked(col, col)


def split3(row):
    high = row.astype(BF16).astype(F32)
    rest = row - high
    mid = rest.astype(BF16).astype(F32)
    low = rest - mid
    return stacked(high, mid, low, jnp.zeros((13, LANES), F32)).astype(BF16)


def kernel(
    dims,
    rhs,
    u_hbm,
    v_hbm,
    ranks,
    assign,
    out,
    phi_out,
    d_out,
    v_own,
    u_fac,
    v_fac,
    u_tr,
    v_tr,
    coeffs,
    d_full,
    x_send,
    x_recv,
    y_own,
    y_send,
    y_recv,
    z_acc,
    z_send,
    z_recv,
    v_full,
    gathered0,
    gathered1,
    picked,
    sib_recv,
    natural,
    cols,
    pair_send,
    pair_recv,
    row_send,
    row_recv,
    zrow_send,
    zrow_recv,
    fac_sem,
    send,
    recv,
    ag_r,
    fw_r,
    xs_r,
    zs_r,
    zg_r,
    ng_r,
    sib_r,
):
    chips, nx, ny, nz, tile_cols, sources = dims
    rows = 2 * sources
    zrows = rows // nz
    gathered = (gathered0, gathered1)
    me_c, me_z = lax.axis_index("col"), lax.axis_index("row")
    chip, core = lax.div(me_c, 2), lax.rem(me_c, 2)
    cx, cy = lax.div(chip, ny), lax.rem(chip, ny)
    sibling = chip * 2 + 1 - core

    def hops(q):
        return min(q // ny, nx - q // ny) + min(q % ny, ny - q % ny)

    near = sorted(range(chips), key=hops)
    far = near[::-1]

    def chip_to(q):
        return lax.rem(cx + lax.div(q, ny), nx) * ny + lax.rem(cy + lax.rem(q, ny), ny)

    def chip_from(q):
        return lax.rem(cx + nx - lax.div(q, ny), nx) * ny + lax.rem(cy + ny - lax.rem(q, ny), ny)

    def along_z(k):
        return lax.rem(me_z + k, nz)

    def remote(src, dst, send, recv, col, row):
        return pltpu.make_async_remote_copy(
            src_ref=src, dst_ref=dst, send_sem=send, recv_sem=recv,
            device_id=(col, row), device_id_type=MESH,
        )

    def copy_ag(rd, q):
        own = d_full.at[rd, chip, core]
        return remote(own, own, send.at[0], ag_r.at[q], chip_to(q) * 2 + core, me_z)

    def copy_fw(rd, q):
        here = d_full.at[rd, chip_from(q), core]
        return remote(here, here, send.at[1], fw_r.at[q], sibling, me_z)

    def copy_xs(rd, q):
        i = chip_to(q)
        return remote(
            x_send.at[rd, i], x_recv.at[rd, i], send.at[2], xs_r.at[q], sibling, me_z
        )

    def copy_ys(rd, q):
        i = chip_to(q)
        return remote(
            y_send.at[rd, i], y_recv.at[rd, q], send.at[3], recv.at[3], i * 2 + core, me_z
        )

    def copy_pair(rd):
        return remote(
            pair_send.at[rd], pair_recv.at[rd], send.at[4], recv.at[4], sibling, me_z
        )

    def copy_row(q):
        return remote(
            row_send, row_recv.at[q], send.at[5], recv.at[5], chip_to(q) * 2 + core, me_z
        )

    def copy_zrow(rd, k):
        return remote(
            zrow_send.at[rd], zrow_recv.at[rd, k], send.at[6], recv.at[6], me_c, along_z(k)
        )

    def copy_zs(rd, k, p):
        return remote(
            z_send.at[rd, along_z(k), p], z_recv.at[rd, k, p], send.at[7], zs_r.at[p], me_c,
            along_z(k),
        )

    def copy_zg(rd, k, p):
        own = v_full.at[rd, me_z, p]
        return remote(own, own, send.at[8], zg_r.at[p], me_c, along_z(k))

    def copy_ng(rd, q):
        own = gathered[rd].at[pl.ds(chip * tile_cols, tile_cols)]
        return remote(own, own, send.at[9 + 3 * rd], ng_r.at[rd], chip_to(q) * 2 + core, me_z)

    def copy_sib(rd):
        return remote(
            picked.at[rd, 1 - core], sib_recv.at[rd], send.at[10], sib_r.at[rd], sibling, me_z
        )

    def copy_nz(rd, k):
        own = natural.at[rd, me_z]
        return remote(own, own, send.at[11], recv.at[11], me_c, along_z(k))

    def arrived(ref, sem):
        remote(ref, ref, sem, sem, sibling, me_z).wait_recv()

    def has_left(ref, sem):
        remote(ref, ref, sem, sem, sibling, me_z).wait_send()

    def loop(low, high, body):
        lax.fori_loop(low, high, lambda i, c: (body(i), c)[1], 0)

    def factor_copies(g):
        some = pl.ds(g * LOAD, LOAD)
        return (
            pltpu.make_async_copy(v_hbm.at[some], v_fac.at[some], fac_sem.at[2 * g]),
            pltpu.make_async_copy(u_hbm.at[some], u_fac.at[some], fac_sem.at[2 * g + 1]),
        )

    lane = lax.broadcasted_iota(jnp.int32, (rows, LANES), 1)

    def masked(value, i, p):
        return jnp.where(lane < ranks[p, i], value, 0.0).astype(BF16)

    def lane_sums(square, acc):
        for at in range(0, square.shape[1], LANES):
            part = square[:, at : at + LANES]
            acc = acc + part[:sources] + part[sources:]
        return acc

    def transpose(fac, held, i):
        for p in range(tile_cols):
            for c in range(2):
                held[i, p, c * LANES : (c + 1) * LANES] = fac[i, p, c].T

    def start_factor(g):
        for copy in factor_copies(g):
            copy.start()

    loop(0, chips // LOAD, start_factor)
    d_full[0, chip, core] = rhs[...].astype(BF16)

    barrier = pltpu.get_barrier_semaphore()

    def greet(col, row):
        pl.semaphore_signal(barrier, inc=1, device_id=(col, row), device_id_type=MESH)

    greet(sibling, me_z)
    for k in range(1, nz):
        greet(me_c, along_z(k))
    loop(1, chips, lambda q: greet(chip_to(q) * 2 + core, me_z))
    pl.semaphore_wait(barrier, chips - 1 + 1 + nz - 1)

    def send_data(rd):
        copy_fw(rd, 0).start()
        for q in far[:-1]:
            copy_ag(rd, q).start()

    send_data(0)

    def ready(g):
        for copy in factor_copies(g):
            copy.wait()
        for i in range(LOAD):
            transpose(v_fac, v_tr, g * LOAD + i)

    loop(0, chips // LOAD, ready)

    def adjoint(rd):
        def pass_on(q):
            copy_ag(rd, q).wait_recv()
            copy_fw(rd, q).start()

        for q in near[1 : AHEAD * GROUP]:
            pass_on(q)

        acc = jnp.zeros((sources, LANES), F32)
        for g in range(chips // GROUP):
            for q in near[(g + AHEAD) * GROUP : (g + AHEAD + 1) * GROUP]:
                pass_on(q)
            for q in near[g * GROUP : (g + 1) * GROUP]:
                i = chip_from(q)
                copy_fw(rd, q).wait_recv()
                data = lanes(d_full[rd, i, 0], d_full[rd, i, 1])
                wide = data.astype(F32)
                acc = lane_sums(wide * wide, acc)
                left = times_conj_factor(data)
                right = lanes(*[u_fac[i, p].reshape(-1, LANES) for p in range(tile_cols)])
                raw = nn(left, right)
                for p in range(tile_cols):
                    coeff = masked(raw[:, p * LANES : (p + 1) * LANES], i, p)
                    coeffs[p, i] = times_conj_factor(coeff)
        zrow_start(rd, to_row(acc))
        if rd == 1:
            loop(1, chips, lambda q: copy_ng(0, q).start())

        def column(p):
            left = lanes(*[coeffs[p, i] for i in range(chips)])
            z = nn(left, stacked(*[v_tr[i, p] for i in range(chips)]))
            z_acc[p] = z
            for r in range(nz):
                z_send[rd, r, p] = z[r * zrows : (r + 1) * zrows].astype(BF16)
            for k in range(1, nz):
                copy_zs(rd, k, p).start()

        for p in range(tile_cols):
            column(p)

    def zrow_start(rd, row):
        zrow_send[rd] = row
        for k in range(1, nz):
            copy_zrow(rd, k).start()

    def zrow_sum(rd):
        total = zrow_send[rd]
        arrived(zrow_recv.at[rd, pl.ds(1, nz - 1)], recv.at[6])
        for k in range(1, nz):
            total = total + zrow_recv[rd, k]
        return total

    own_rows = pl.ds(pl.multiple_of(me_z * zrows, zrows), zrows)

    def own_col(slot):
        part = cols[slot, own_rows, :]
        return lanes(part, part)

    def model(rd, finish):
        for p in range(tile_cols):
            total = z_acc[p, own_rows, :]
            arrived(z_recv.at[rd, pl.ds(1, nz - 1), p], zs_r.at[p])
            for k in range(1, nz):
                total = total + z_recv[rd, k, p].astype(F32)
            v_hat = finish(total, p)
            v_own[rd, p] = v_hat
            v_b = v_hat.astype(BF16)
            v_full[rd, me_z, p] = v_b
            for k in range(1, nz):
                copy_zg(rd, k, p).start()
            gathered[rd][chip * tile_cols + p] = v_b
        if rd == 1:
            loop(1, chips, lambda q: copy_ng(1, q).start())

    def forward(rd):
        acc = jnp.zeros((sources, LANES), F32)
        for p in range(tile_cols):
            arrived(v_full.at[rd, pl.ds(0, nz - 1), p], zg_r.at[p])
            vec = stacked(*[v_full[rd, r, p] for r in range(nz)])
            wide = vec.astype(F32)
            acc = lane_sums(wide * wide, acc)
            left = times_factor(vec)

            def group(g, left=left, p=p):
                some = min(UNROLL, chips)
                for h in range(some // 2):
                    where = [g * some + h * 2 + j for j in range(2)]
                    right = lanes(*[v_fac[i, p].reshape(-1, LANES) for i in where])
                    raw = nn(left, right)
                    for j, i in enumerate(where):
                        coeff = masked(raw[:, j * LANES : (j + 1) * LANES], i, p)
                        coeffs[p, i] = times_factor(coeff)

            loop(0, chips // min(UNROLL, chips), group)
        own = to_row(acc)
        pair_send[rd] = own
        copy_pair(rd).start()

        def compute(g):
            for q in far[g * GROUP : (g + 1) * GROUP]:
                i = chip_to(q)
                left = lanes(*[coeffs[p, i] for p in range(tile_cols)])
                y = nn(left, stacked(*[u_tr[i, p] for p in range(tile_cols)]))
                zero, one = y[:, :LANES], y[:, LANES:]
                y_own[i] = jnp.where(core == 0, zero, one)
                x_send[rd, i] = jnp.where(core == 0, one, zero).astype(BF16)
                copy_xs(rd, q).start()

        def finish(g, block):
            for q in far[g * GROUP : (g + 1) * GROUP]:
                i = chip_to(q)
                copy_xs(rd, q).wait_recv()
                y_send[rd, i, :rows] = (y_own[i] + x_recv[rd, i].astype(F32)).astype(BF16)
                y_send[rd, i, rows:] = block

                if q > 0:
                    copy_ys(rd, q).start()

        behind = min(BEHIND, chips // GROUP)
        for g in range(behind):
            compute(g)
        copy_pair(rd).wait_recv()
        block = split3(own + pair_recv[rd])

        for g in range(behind, chips // GROUP):
            compute(g)
            finish(g - behind, block)
        for g in range(chips // GROUP - behind, chips // GROUP):
            finish(g, block)

    def data_sum(rd):
        total = y_send[rd, chip].astype(F32)
        arrived(y_recv.at[rd, pl.ds(1, chips - 1)], recv.at[3])
        for q in range(1, chips):
            total = total + y_recv[rd, q].astype(F32)
        row = total[rows : rows + 1] + total[rows + 1 : rows + 2] + total[rows + 2 : rows + 3]
        return total[:rows], row

    def pick(rd, held):
        arrived(gathered[rd].at[pl.ds(0, (chips - 1) * tile_cols)], ng_r.at[rd])
        for j, (found, at) in enumerate(held):
            seg = gathered[rd][at].astype(F32) * found.astype(F32)
            picked[rd, j // tile_cols, j % tile_cols] = seg.astype(BF16)
        copy_sib(rd).start()

    def join(rd):
        copy_sib(rd).wait_recv()
        mine = picked[rd, core].astype(F32) + sib_recv[rd].astype(F32)
        natural[rd, me_z] = mine.astype(BF16)
        for k in range(1, nz):
            copy_nz(rd, k).start()

    def find_held():
        first = chip * (2 * tile_cols)
        zero = jnp.int32(0)

        def step(a, carry):
            found, at = list(carry[0]), list(carry[1])
            for t in range(tile_cols):
                held = assign[a * (2 * tile_cols) + core * tile_cols + t] - first
                for j in range(2 * tile_cols):
                    hit = held == j
                    found[j] = jnp.where(hit, 1, found[j])
                    at[j] = jnp.where(hit, a * tile_cols + t, at[j])
            return tuple(found), tuple(at)

        many = 2 * tile_cols
        found, at = lax.fori_loop(0, chips, step, ((zero,) * many, (zero,) * many))
        return list(zip(found, at))

    adjoint(0)
    def transpose_some(g):
        for i in range(4):
            transpose(u_fac, u_tr, g * 4 + i)

    loop(0, chips // 4, transpose_some)
    beta0 = jnp.sqrt(zrow_sum(0))
    cols[0] = to_col(beta0, sources)
    by_beta = own_col(0)
    model(0, lambda total, p: total / by_beta)

    forward(0)
    held = find_held()
    y, alpha0 = data_sum(0)
    alpha0 = jnp.sqrt(alpha0)
    cols[1] = to_col(alpha0, sources)
    d_hat = y / cols[1] - cols[1] * (rhs[...] / cols[0])
    d_full[1, chip, core] = d_hat.astype(BF16)
    send_data(1)
    d_out[...] = d_hat
    adjoint(1)
    beta1 = jnp.sqrt(zrow_sum(1))
    cols[2] = to_col(beta1, sources)
    beta, alpha = own_col(2), own_col(1)
    model(1, lambda total, p: total / beta - beta * (v_own[0, p] / alpha))

    pick(0, held)
    forward(1)
    join(0)
    pick(1, held)
    y, alpha1 = data_sum(1)
    alpha1 = jnp.sqrt(alpha1)
    cols[3] = to_col(alpha1, sources)
    d_hat = y / cols[3] - cols[3] * (d_out[...] / cols[2])
    square = d_hat * d_hat
    own = to_row(square[:sources] + square[sources:])
    pair_send[2] = own
    copy_pair(2).start()
    d_out[...] = d_hat
    join(1)
    copy_pair(2).wait_recv()
    row_send[...] = own + pair_recv[2]
    loop(1, chips, lambda q: copy_row(q).start())
    rho1 = jnp.sqrt(alpha0 * alpha0 + beta1 * beta1)
    cosine = alpha0 / rho1
    sine = beta1 / rho1
    theta = sine * alpha1
    rhobar = -cosine * alpha1
    phi1 = cosine * beta0
    phibar = sine * beta0
    total = row_send[...]
    arrived(row_recv.at[pl.ds(1, chips - 1)], recv.at[5])
    for q in range(1, chips):
        total = total + row_recv[q]
    zrow_start(2, total)
    arrived(natural.at[:, pl.ds(0, nz - 1)], recv.at[11])
    beta2 = jnp.sqrt(zrow_sum(2))
    rho2 = jnp.sqrt(rhobar * rhobar + beta2 * beta2)
    cosine = rhobar / rho2
    sine = beta2 / rho2
    step2 = cosine * phibar / rho2
    phi_out[0:1] = sine * phibar
    phi_out[1:2] = sine / rho2
    phi_out[2:3] = theta / rho1
    phi_out[3:4] = alpha0
    phi_out[4:5] = alpha1
    first = to_col((phi1 / rho1 - step2 * (theta / rho1)) / alpha0, sources)
    second = to_col(step2 / alpha1, sources)
    width = natural.shape[-1]
    for p in range(tile_cols):
        for at in range(0, width, LANES):
            one = stacked(*[natural[0, r, p, :, at : at + LANES] for r in range(nz)])
            two = stacked(*[natural[1, r, p, :, at : at + LANES] for r in range(nz)])
            out[:, p * width + at : p * width + at + LANES] = (
                first * one.astype(F32) + second * two.astype(F32)
            )

    others, zs = pl.ds(1, chips - 1), pl.ds(1, nz - 1)
    has_left(d_full.at[:, others, 0], send.at[0])
    has_left(d_full.at[:, :, 0], send.at[1])
    has_left(x_send, send.at[2])
    has_left(y_send.at[:, others], send.at[3])
    has_left(pair_send, send.at[4])
    has_left(row_recv.at[others], send.at[5])
    has_left(zrow_recv.at[:, zs], send.at[6])
    has_left(z_send.at[:, zs], send.at[7])
    has_left(v_full.at[:, zs], send.at[8])
    for rd in range(2):
        has_left(gathered[rd].at[pl.ds(0, (chips - 1) * tile_cols)], send.at[9 + 3 * rd])
    has_left(picked.at[0], send.at[10])
    has_left(natural.at[:, zs], send.at[11])


def last_adjoint(d_hat, v_hats, scalars, u_factor, v_factor, ranks):
    tile_rows, tile_cols, _, tile_size, rank_cap = u_factor.shape
    sources = d_hat.shape[0] // 2
    rank_iota = lax.broadcasted_iota(jnp.int32, (tile_rows, tile_cols, 1, 1, rank_cap), 4)
    mask = (rank_iota < ranks[:, :, None, None, None]).astype(F32)
    d_hat = d_hat.reshape(2, sources, -1)
    beta = jnp.sqrt(lax.psum(jnp.sum(d_hat * d_hat, axis=(0, 2)), ("col", "row")))
    data = lax.all_gather(d_hat.astype(BF16), "col", axis=2, tiled=True)
    data = data.reshape(2, sources, tile_rows, tile_size)
    raw = jnp.einsum("ipcnk,dsin->ipcdsk", u_factor, data, preferred_element_type=F32)
    coeff = jnp.stack([raw[:, :, 0, 0] + raw[:, :, 1, 1], raw[:, :, 0, 1] - raw[:, :, 1, 0]], axis=2)
    coeff = (coeff * mask).astype(BF16)
    prod = jnp.einsum("ipcnk,ipdsk->cdspn", v_factor, coeff, preferred_element_type=F32)
    model = jnp.stack([prod[0, 0] + prod[1, 1], prod[0, 1] - prod[1, 0]], axis=0)
    model = lax.psum(model, "row").reshape(2, sources, tile_cols * tile_size)
    sine_by_rho, theta_by_rho, alpha0, alpha1 = [row[None, :, None] for row in scalars]
    v_hats = lax.all_gather(v_hats, "row", axis=2, tiled=True)
    v_hats = v_hats.transpose(0, 2, 1, 3).reshape(2, *model.shape)
    v_prev = v_hats[1] / alpha1
    w_prev = v_prev - theta_by_rho * (v_hats[0] / alpha0)
    v_hat = model / beta[None, :, None] - beta[None, :, None] * v_prev
    alpha = jnp.sqrt(lax.psum(jnp.sum(v_hat * v_hat, axis=(0, 2)), "col"))
    v_vec = v_hat / alpha[None, :, None]
    return v_vec, alpha, v_vec - sine_by_rho * alpha[None, :, None] * w_prev


def on_device(nz, rhs, u_factor, v_factor, ranks, assign):
    tile_rows, tile_cols, _, tile_size, _ = u_factor.shape
    sources = rhs.shape[1]
    rows = 2 * sources
    zrows = rows // nz
    chips = tile_rows
    ny = math.isqrt(chips)
    nx = chips // ny
    dims = (chips, nx, ny, nz, tile_cols, sources)
    seg = (tile_cols, zrows, tile_size)
    dma = pltpu.SemaphoreType.DMA
    vmem = pl.BlockSpec(memory_space=pltpu.VMEM)
    smem = pl.BlockSpec(memory_space=pltpu.SMEM)
    hbm = pl.BlockSpec(memory_space=pl.ANY)
    out, scalars, d_hat, v_hats = pl.pallas_call(
        functools.partial(kernel, dims),
        out_shape=[
            jax.ShapeDtypeStruct((rows, tile_cols * tile_size), F32),
            jax.ShapeDtypeStruct((5, LANES), F32),
            jax.ShapeDtypeStruct((rows, LANES), F32),
            jax.ShapeDtypeStruct((2, *seg), F32),
        ],
        in_specs=[vmem, hbm, hbm, smem, smem],
        out_specs=[vmem] * 4,
        scratch_shapes=[
            pltpu.VMEM(u_factor.shape, BF16),
            pltpu.VMEM(v_factor.shape, BF16),
            pltpu.VMEM((chips, tile_cols, 2 * LANES, tile_size), BF16),
            pltpu.VMEM((chips, tile_cols, 2 * LANES, tile_size), BF16),
            pltpu.VMEM((tile_cols, chips, rows, 2 * LANES), BF16),
            pltpu.VMEM((2, chips, 2, rows, LANES), BF16),
            pltpu.VMEM((2, chips, rows, LANES), BF16),
            pltpu.VMEM((2, chips, rows, LANES), BF16),
            pltpu.VMEM((chips, rows, LANES), F32),
            pltpu.VMEM((2, chips, rows + 16, LANES), BF16),
            pltpu.VMEM((2, chips, rows + 16, LANES), BF16),
            pltpu.VMEM((tile_cols, rows, tile_size), F32),
            pltpu.VMEM((2, nz, *seg), BF16),
            pltpu.VMEM((2, nz, *seg), BF16),
            pltpu.VMEM((2, nz, *seg), BF16),
            pltpu.VMEM((chips * tile_cols, zrows, tile_size), BF16),
            pltpu.VMEM((chips * tile_cols, zrows, tile_size), BF16),
            pltpu.VMEM((2, 2, *seg), BF16),
            pltpu.VMEM((2, *seg), BF16),
            pltpu.VMEM((2, nz, *seg), BF16),
            pltpu.VMEM((4, rows, LANES), F32),
            pltpu.VMEM((3, 1, LANES), F32),
            pltpu.VMEM((3, 1, LANES), F32),
            pltpu.VMEM((1, LANES), F32),
            pltpu.VMEM((chips, 1, LANES), F32),
            pltpu.VMEM((3, 1, LANES), F32),
            pltpu.VMEM((3, nz, 1, LANES), F32),
            dma((chips,)),
            dma((13,)), dma((12,)),
            dma((chips,)), dma((chips,)), dma((chips,)),
            dma((tile_cols,)), dma((tile_cols,)),
            dma((2,)), dma((2,)),
        ],
        compiler_params=pltpu.CompilerParams(
            collective_id=0, has_side_effects=True, vmem_limit_bytes=60 * 2**20
        ),
        name="lsqr",
    )(rhs.reshape(rows, LANES), u_factor, v_factor, ranks.T, assign)
    last_adjoint(d_hat, v_hats, scalars[1:, :sources], u_factor, v_factor, ranks)
    phibar = scalars[0, :sources]
    return out.reshape(2, sources, tile_cols * tile_size), phibar


def solution(mesh):
    return jax.shard_map(
        functools.partial(on_device, mesh.shape["row"]),
        mesh=mesh,
        in_specs=(
            P(None, None, "row", "col"),
            P("row", "col", None, None, None),
            P("row", "col", None, None, None),
            P("row", "col"),
            P(),
        ),
        out_specs=(P(None, None, "col"), P()),
        check_vma=False,
    )
```

```python
import functools
import math

import jax
import jax.numpy as jnp
from jax import lax
from jax.experimental import pallas as pl
from jax.experimental.pallas import tpu as pltpu
from jax.sharding import PartitionSpec as P

F32 = jnp.float32
BF16 = jnp.bfloat16
MESH = pl.DeviceIdType.MESH
LANES = 128
GROUP = 2
LOAD = 2
AHEAD = 2
UNROLL = 16
BEHIND = 2


def nn(lhs, rhs):
    return jnp.dot(lhs, rhs, preferred_element_type=F32)


def nt(lhs, rhs):
    return lax.dot_general(lhs, rhs, (((1,), (1,)), ((), ())), preferred_element_type=F32)


def lanes(*parts):
    return jnp.concatenate(parts, axis=1)


def stacked(*parts):
    return jnp.concatenate(parts, axis=0)


def times_factor(vec):
    half = vec.shape[0] // 2
    re, im = vec[:half], vec[half:]
    return stacked(lanes(re, -im), lanes(im, re))


def times_conj_factor(vec):
    half = vec.shape[0] // 2
    re, im = vec[:half], vec[half:]
    return stacked(lanes(re, im), lanes(im, -re))


def to_row(acc):
    pad = jnp.zeros((LANES - acc.shape[0], LANES), F32)
    return jnp.sum(stacked(acc, pad).T, axis=0, keepdims=True)


def to_col(row, sources):
    col = jnp.broadcast_to(row, (LANES, LANES)).T[:sources]
    return stacked(col, col)


def split3(row):
    high = row.astype(BF16).astype(F32)
    rest = row - high
    mid = rest.astype(BF16).astype(F32)
    low = rest - mid
    return stacked(high, mid, low, jnp.zeros((13, LANES), F32)).astype(BF16)


def kernel(
    dims,
    rhs,
    u_hbm,
    v_hbm,
    ranks,
    assign,
    nat_out,
    phi_out,
    d_out,
    v_own,
    u_fac,
    v_fac,
    u_tr,
    v_tr,
    coeffs,
    d_full,
    x_send,
    x_recv,
    y_own,
    y_send,
    y_recv,
    z_acc,
    z_send,
    z_recv,
    v_full,
    gathered0,
    gathered1,
    picked,
    sib_recv,
    natural,
    cols,
    pair_send,
    pair_recv,
    row_send,
    row_recv,
    zrow_send,
    zrow_recv,
    last_send,
    last_recv,
    fac_sem,
    send,
    recv,
    ag_r,
    fw_r,
    xs_r,
    zs_r,
    zg_r,
    ng_r,
    sib_r,
):
    chips, nx, ny, nz, tile_cols, sources = dims
    rows = 2 * sources
    zrows = rows // nz
    gathered = (gathered0, gathered1)
    me_c, me_z = lax.axis_index("col"), lax.axis_index("row")
    chip, core = lax.div(me_c, 2), lax.rem(me_c, 2)
    cx, cy = lax.div(chip, ny), lax.rem(chip, ny)
    sibling = chip * 2 + 1 - core

    def hops(q):
        return min(q // ny, nx - q // ny) + min(q % ny, ny - q % ny)

    near = sorted(range(chips), key=hops)
    far = near[::-1]

    def chip_to(q):
        return lax.rem(cx + lax.div(q, ny), nx) * ny + lax.rem(cy + lax.rem(q, ny), ny)

    def chip_from(q):
        return lax.rem(cx + nx - lax.div(q, ny), nx) * ny + lax.rem(cy + ny - lax.rem(q, ny), ny)

    def along_z(k):
        return lax.rem(me_z + k, nz)

    def remote(src, dst, send, recv, col, row):
        return pltpu.make_async_remote_copy(
            src_ref=src, dst_ref=dst, send_sem=send, recv_sem=recv,
            device_id=(col, row), device_id_type=MESH,
        )

    def copy_ag(rd, q):
        own = d_full.at[rd, chip, core]
        return remote(own, own, send.at[0], ag_r.at[q], chip_to(q) * 2 + core, me_z)

    def copy_fw(rd, q):
        here = d_full.at[rd, chip_from(q), core]
        return remote(here, here, send.at[1], fw_r.at[q], sibling, me_z)

    def copy_xs(rd, q):
        i = chip_to(q)
        return remote(
            x_send.at[rd, i], x_recv.at[rd, i], send.at[2], xs_r.at[q], sibling, me_z
        )

    def copy_ys(rd, q):
        i = chip_to(q)
        return remote(
            y_send.at[rd, i], y_recv.at[rd, q], send.at[3], recv.at[3], i * 2 + core, me_z
        )

    def copy_pair(rd):
        return remote(
            pair_send.at[rd], pair_recv.at[rd], send.at[4], recv.at[4], sibling, me_z
        )

    def copy_row(q):
        return remote(
            row_send, row_recv.at[q], send.at[5], recv.at[5], chip_to(q) * 2 + core, me_z
        )

    def copy_zrow(rd, k):
        return remote(
            zrow_send.at[rd], zrow_recv.at[rd, k], send.at[6], recv.at[6], me_c, along_z(k)
        )

    def beside(m):
        return chip * 2 + lax.rem(core + m % 2, 2), along_z(m // 2)

    def copy_last(m):
        return remote(last_send, last_recv.at[m], send.at[13], recv.at[12], *beside(m))

    def copy_zs(rd, k, p):
        return remote(
            z_send.at[rd, along_z(k), p], z_recv.at[rd, k, p], send.at[7], zs_r.at[p], me_c,
            along_z(k),
        )

    def copy_zg(rd, k, p):
        own = v_full.at[rd, me_z, p]
        return remote(own, own, send.at[8], zg_r.at[p], me_c, along_z(k))

    def copy_ng(rd, q):
        own = gathered[rd].at[pl.ds(chip * tile_cols, tile_cols)]
        return remote(own, own, send.at[9 + 3 * rd], ng_r.at[rd], chip_to(q) * 2 + core, me_z)

    def copy_sib(rd):
        return remote(
            picked.at[rd, 1 - core], sib_recv.at[rd], send.at[10], sib_r.at[rd], sibling, me_z
        )

    def copy_nz(rd, k):
        own = natural.at[rd, me_z]
        return remote(own, own, send.at[11], recv.at[11], me_c, along_z(k))

    def arrived(ref, sem):
        remote(ref, ref, sem, sem, sibling, me_z).wait_recv()

    def has_left(ref, sem):
        remote(ref, ref, sem, sem, sibling, me_z).wait_send()

    def loop(low, high, body):
        lax.fori_loop(low, high, lambda i, c: (body(i), c)[1], 0)

    def factor_copies(g):
        some = pl.ds(g * LOAD, LOAD)
        return (
            pltpu.make_async_copy(v_hbm.at[some], v_fac.at[some], fac_sem.at[2 * g]),
            pltpu.make_async_copy(u_hbm.at[some], u_fac.at[some], fac_sem.at[2 * g + 1]),
        )

    lane = lax.broadcasted_iota(jnp.int32, (rows, LANES), 1)

    def masked(value, i, p):
        return jnp.where(lane < ranks[p, i], value, 0.0).astype(BF16)

    def lane_sums(square, acc):
        for at in range(0, square.shape[1], LANES):
            part = square[:, at : at + LANES]
            acc = acc + part[:sources] + part[sources:]
        return acc

    def transpose(fac, held, i):
        for p in range(tile_cols):
            for c in range(2):
                held[i, p, c * LANES : (c + 1) * LANES] = fac[i, p, c].T

    def start_factor(g):
        for copy in factor_copies(g):
            copy.start()

    loop(0, chips // LOAD, start_factor)
    d_full[0, chip, core] = rhs[...].astype(BF16)

    barrier = pltpu.get_barrier_semaphore()

    def greet(col, row):
        pl.semaphore_signal(barrier, inc=1, device_id=(col, row), device_id_type=MESH)

    for m in range(1, 2 * nz):
        greet(*beside(m))
    loop(1, chips, lambda q: greet(chip_to(q) * 2 + core, me_z))
    pl.semaphore_wait(barrier, chips - 1 + 2 * nz - 1)

    def send_data(rd):
        copy_fw(rd, 0).start()
        for q in far[:-1]:
            copy_ag(rd, q).start()

    send_data(0)

    def ready(g):
        for copy in factor_copies(g):
            copy.wait()
        for i in range(LOAD):
            transpose(v_fac, v_tr, g * LOAD + i)

    loop(0, chips // LOAD, ready)

    def adjoint(rd):
        def pass_on(q):
            copy_ag(rd, q).wait_recv()
            copy_fw(rd, q).start()

        for q in near[1 : AHEAD * GROUP]:
            pass_on(q)

        acc = jnp.zeros((sources, LANES), F32)
        for g in range(chips // GROUP):
            for q in near[(g + AHEAD) * GROUP : (g + AHEAD + 1) * GROUP]:
                pass_on(q)
            for q in near[g * GROUP : (g + 1) * GROUP]:
                i = chip_from(q)
                copy_fw(rd, q).wait_recv()
                data = lanes(d_full[rd, i, 0], d_full[rd, i, 1])
                wide = data.astype(F32)
                acc = lane_sums(wide * wide, acc)
                left = times_conj_factor(data)
                right = lanes(*[u_fac[i, p].reshape(-1, LANES) for p in range(tile_cols)])
                raw = nn(left, right)
                for p in range(tile_cols):
                    coeff = masked(raw[:, p * LANES : (p + 1) * LANES], i, p)
                    coeffs[p, i] = times_conj_factor(coeff)
            some = [chip_from(q) for q in near[g * GROUP : (g + 1) * GROUP]]
            last = g == chips // GROUP - 1
            if last:
                zrow_start(rd, to_row(acc))
            for p in range(tile_cols):
                left = lanes(*[coeffs[p, i] for i in some])
                z = nn(left, stacked(*[v_tr[i, p] for i in some]))
                if g > 0:
                    z += z_acc[p]
                z_acc[p] = z
                if last:
                    for r in range(nz):
                        z_send[rd, r, p] = z[r * zrows : (r + 1) * zrows].astype(BF16)
                    for k in range(1, nz):
                        copy_zs(rd, k, p).start()

    def zrow_start(rd, row):
        zrow_send[rd] = row
        for k in range(1, nz):
            copy_zrow(rd, k).start()

    def zrow_sum(rd):
        total = zrow_send[rd]
        arrived(zrow_recv.at[rd, pl.ds(1, nz - 1)], recv.at[6])
        for k in range(1, nz):
            total = total + zrow_recv[rd, k]
        return total

    own_rows = pl.ds(pl.multiple_of(me_z * zrows, zrows), zrows)

    def own_col(slot):
        part = cols[slot, own_rows, :]
        return lanes(part, part)

    def model(rd, finish):
        for p in range(tile_cols):
            total = z_acc[p, own_rows, :]
            arrived(z_recv.at[rd, pl.ds(1, nz - 1), p], zs_r.at[p])
            for k in range(1, nz):
                total = total + z_recv[rd, k, p].astype(F32)
            v_hat = finish(total, p)
            v_own[rd, p] = v_hat
            v_b = v_hat.astype(BF16)
            v_full[rd, me_z, p] = v_b
            for k in range(1, nz):
                copy_zg(rd, k, p).start()
            gathered[rd][chip * tile_cols + p] = v_b
        loop(1, chips, lambda q: copy_ng(rd, q).start())

    def forward(rd):
        acc = jnp.zeros((sources, LANES), F32)
        for p in range(tile_cols):
            arrived(v_full.at[rd, pl.ds(0, nz - 1), p], zg_r.at[p])
            vec = stacked(*[v_full[rd, r, p] for r in range(nz)])
            wide = vec.astype(F32)
            acc = lane_sums(wide * wide, acc)
            left = times_factor(vec)

            def group(g, left=left, p=p):
                some = min(UNROLL, chips)
                for h in range(some // 2):
                    where = [g * some + h * 2 + j for j in range(2)]
                    right = lanes(*[v_fac[i, p].reshape(-1, LANES) for i in where])
                    raw = nn(left, right)
                    for j, i in enumerate(where):
                        coeff = masked(raw[:, j * LANES : (j + 1) * LANES], i, p)
                        coeffs[p, i] = times_factor(coeff)

            loop(0, chips // min(UNROLL, chips), group)
        own = to_row(acc)
        pair_send[rd] = own
        copy_pair(rd).start()

        def compute(g):
            for q in far[g * GROUP : (g + 1) * GROUP]:
                i = chip_to(q)
                left = lanes(*[coeffs[p, i] for p in range(tile_cols)])
                y = nn(left, stacked(*[u_tr[i, p] for p in range(tile_cols)]))
                zero, one = y[:, :LANES], y[:, LANES:]
                y_own[i] = jnp.where(core == 0, zero, one)
                x_send[rd, i] = jnp.where(core == 0, one, zero).astype(BF16)
                copy_xs(rd, q).start()

        def finish(g, block):
            for q in far[g * GROUP : (g + 1) * GROUP]:
                i = chip_to(q)
                copy_xs(rd, q).wait_recv()
                y_send[rd, i, :rows] = (y_own[i] + x_recv[rd, i].astype(F32)).astype(BF16)
                y_send[rd, i, rows:] = block

                if q > 0:
                    copy_ys(rd, q).start()

        behind = min(BEHIND, chips // GROUP)
        for g in range(behind):
            compute(g)
        copy_pair(rd).wait_recv()
        block = split3(own + pair_recv[rd])

        for g in range(behind, chips // GROUP):
            compute(g)
            finish(g - behind, block)
        for g in range(chips // GROUP - behind, chips // GROUP):
            finish(g, block)

    def data_sum(rd):
        total = y_send[rd, chip].astype(F32)
        arrived(y_recv.at[rd, pl.ds(1, chips - 1)], recv.at[3])
        for q in range(1, chips):
            total = total + y_recv[rd, q].astype(F32)
        row = total[rows : rows + 1] + total[rows + 1 : rows + 2] + total[rows + 2 : rows + 3]
        return total[:rows], row

    def pick(rd, held):
        arrived(gathered[rd].at[pl.ds(0, (chips - 1) * tile_cols)], ng_r.at[rd])
        for j, (found, at) in enumerate(held):
            seg = gathered[rd][at].astype(F32) * found.astype(F32)
            picked[rd, j // tile_cols, j % tile_cols] = seg.astype(BF16)
        copy_sib(rd).start()

    def join(rd):
        copy_sib(rd).wait_recv()
        mine = picked[rd, core].astype(F32) + sib_recv[rd].astype(F32)
        natural[rd, me_z] = mine.astype(BF16)
        for k in range(1, nz):
            copy_nz(rd, k).start()

    def find_held():
        first = chip * (2 * tile_cols)
        zero = jnp.int32(0)

        def step(a, carry):
            found, at = list(carry[0]), list(carry[1])
            for t in range(tile_cols):
                held = assign[a * (2 * tile_cols) + core * tile_cols + t] - first
                for j in range(2 * tile_cols):
                    hit = held == j
                    found[j] = jnp.where(hit, 1, found[j])
                    at[j] = jnp.where(hit, a * tile_cols + t, at[j])
            return tuple(found), tuple(at)

        many = 2 * tile_cols
        found, at = lax.fori_loop(0, chips, step, ((zero,) * many, (zero,) * many))
        return list(zip(found, at))

    adjoint(0)
    def transpose_some(g):
        for i in range(4):
            transpose(u_fac, u_tr, g * 4 + i)

    loop(0, chips // 4, transpose_some)
    beta0 = jnp.sqrt(zrow_sum(0))
    cols[0] = to_col(beta0, sources)
    by_beta = own_col(0)
    model(0, lambda total, p: total / by_beta)

    forward(0)
    held = find_held()
    y, alpha0 = data_sum(0)
    alpha0 = jnp.sqrt(alpha0)
    cols[1] = to_col(alpha0, sources)
    d_hat = y / cols[1] - cols[1] * (rhs[...] / cols[0])
    d_full[1, chip, core] = d_hat.astype(BF16)
    send_data(1)
    d_out[...] = d_hat
    adjoint(1)
    beta1 = jnp.sqrt(zrow_sum(1))
    cols[2] = to_col(beta1, sources)
    beta, alpha = own_col(2), own_col(1)
    model(1, lambda total, p: total / beta - beta * (v_own[0, p] / alpha))

    pick(0, held)
    forward(1)
    join(0)
    pick(1, held)
    y, alpha1 = data_sum(1)
    alpha1 = jnp.sqrt(alpha1)
    cols[3] = to_col(alpha1, sources)
    d_hat = y / cols[3] - cols[3] * (d_out[...] / cols[2])
    square = d_hat * d_hat
    own = to_row(square[:sources] + square[sources:])
    row_send[...] = own
    for q in far[:-1]:
        copy_row(q).start()
    d_out[...] = d_hat
    join(1)
    rho1 = jnp.sqrt(alpha0 * alpha0 + beta1 * beta1)
    cosine = alpha0 / rho1
    sine = beta1 / rho1
    theta = sine * alpha1
    rhobar = -cosine * alpha1
    phi1 = cosine * beta0
    phibar = sine * beta0
    total = row_send[...]
    arrived(row_recv.at[pl.ds(1, chips - 1)], recv.at[5])
    for q in range(1, chips):
        total = total + row_recv[q]
    last_send[...] = total
    for m in range(1, 2 * nz):
        copy_last(m).start()
    arrived(natural.at[:, pl.ds(0, nz - 1)], recv.at[11])
    nat_out[...] = natural[...]
    arrived(last_recv.at[pl.ds(1, 2 * nz - 1)], recv.at[12])
    for m in range(1, 2 * nz):
        total = total + last_recv[m]
    beta2 = jnp.sqrt(total)
    rho2 = jnp.sqrt(rhobar * rhobar + beta2 * beta2)
    cosine = rhobar / rho2
    sine = beta2 / rho2
    step2 = cosine * phibar / rho2
    phi_out[...] = jnp.zeros_like(phi_out)
    phi_out[0:1] = sine * phibar
    phi_out[1:2] = sine / rho2
    phi_out[2:3] = theta / rho1
    phi_out[3:4] = alpha0
    phi_out[4:5] = alpha1
    phi_out[5:6] = (phi1 / rho1 - step2 * (theta / rho1)) / alpha0
    phi_out[6:7] = step2 / alpha1

    others, zs = pl.ds(1, chips - 1), pl.ds(1, nz - 1)
    has_left(d_full.at[:, others, 0], send.at[0])
    has_left(d_full.at[:, :, 0], send.at[1])
    has_left(x_send, send.at[2])
    has_left(y_send.at[:, others], send.at[3])
    has_left(pair_send, send.at[4])
    has_left(row_recv.at[others], send.at[5])
    has_left(zrow_recv.at[:, zs], send.at[6])
    has_left(z_send.at[:, zs], send.at[7])
    has_left(v_full.at[:, zs], send.at[8])
    for rd in range(2):
        has_left(gathered[rd].at[pl.ds(0, (chips - 1) * tile_cols)], send.at[9 + 3 * rd])
    has_left(picked.at[0], send.at[10])
    has_left(natural.at[:, zs], send.at[11])
    has_left(last_recv.at[pl.ds(1, 2 * nz - 1)], send.at[13])


def combine(nz, scalars, natural, out, phi):
    sources = phi.shape[1]
    _, _, tile_cols, _, width = natural.shape
    first, second = to_col(scalars[5:6], sources), to_col(scalars[6:7], sources)
    phi[...] = scalars[0:1, :sources]
    for p in range(tile_cols):
        for at in range(0, width, LANES):
            one = stacked(*[natural[0, r, p, :, at : at + LANES] for r in range(nz)])
            two = stacked(*[natural[1, r, p, :, at : at + LANES] for r in range(nz)])
            out[:, p * width + at : p * width + at + LANES] = (
                first * one.astype(F32) + second * two.astype(F32)
            )


def last_adjoint(d_hat, v_hats, scalars, u_factor, v_factor, ranks):
    tile_rows, tile_cols, _, tile_size, rank_cap = u_factor.shape
    sources = d_hat.shape[0] // 2
    rank_iota = lax.broadcasted_iota(jnp.int32, (tile_rows, tile_cols, 1, 1, rank_cap), 4)
    mask = (rank_iota < ranks[:, :, None, None, None]).astype(F32)
    d_hat = d_hat.reshape(2, sources, -1)
    beta = jnp.sqrt(lax.psum(jnp.sum(d_hat * d_hat, axis=(0, 2)), ("col", "row")))
    data = lax.all_gather(d_hat.astype(BF16), "col", axis=2, tiled=True)
    data = data.reshape(2, sources, tile_rows, tile_size)
    raw = jnp.einsum("ipcnk,dsin->ipcdsk", u_factor, data, preferred_element_type=F32)
    coeff = jnp.stack([raw[:, :, 0, 0] + raw[:, :, 1, 1], raw[:, :, 0, 1] - raw[:, :, 1, 0]], axis=2)
    coeff = (coeff * mask).astype(BF16)
    prod = jnp.einsum("ipcnk,ipdsk->cdspn", v_factor, coeff, preferred_element_type=F32)
    model = jnp.stack([prod[0, 0] + prod[1, 1], prod[0, 1] - prod[1, 0]], axis=0)
    model = lax.psum(model, "row").reshape(2, sources, tile_cols * tile_size)
    sine_by_rho, theta_by_rho, alpha0, alpha1 = [row[None, :, None] for row in scalars]
    v_hats = lax.all_gather(v_hats, "row", axis=2, tiled=True)
    v_hats = v_hats.transpose(0, 2, 1, 3).reshape(2, *model.shape)
    v_prev = v_hats[1] / alpha1
    w_prev = v_prev - theta_by_rho * (v_hats[0] / alpha0)
    v_hat = model / beta[None, :, None] - beta[None, :, None] * v_prev
    alpha = jnp.sqrt(lax.psum(jnp.sum(v_hat * v_hat, axis=(0, 2)), "col"))
    v_vec = v_hat / alpha[None, :, None]
    return v_vec, alpha, v_vec - sine_by_rho * alpha[None, :, None] * w_prev


def on_device(nz, rhs, u_factor, v_factor, ranks, assign):
    tile_rows, tile_cols, _, tile_size, _ = u_factor.shape
    sources = rhs.shape[1]
    rows = 2 * sources
    zrows = rows // nz
    chips = tile_rows
    ny = math.isqrt(chips)
    nx = chips // ny
    dims = (chips, nx, ny, nz, tile_cols, sources)
    seg = (tile_cols, zrows, tile_size)
    dma = pltpu.SemaphoreType.DMA
    vmem = pl.BlockSpec(memory_space=pltpu.VMEM)
    smem = pl.BlockSpec(memory_space=pltpu.SMEM)
    hbm = pl.BlockSpec(memory_space=pl.ANY)
    natural, scalars, d_hat, v_hats = pl.pallas_call(
        functools.partial(kernel, dims),
        out_shape=[
            jax.ShapeDtypeStruct((2, nz, *seg), BF16),
            jax.ShapeDtypeStruct((8, LANES), F32),
            jax.ShapeDtypeStruct((rows, LANES), F32),
            jax.ShapeDtypeStruct((2, *seg), F32),
        ],
        in_specs=[vmem, hbm, hbm, smem, smem],
        out_specs=[vmem] * 4,
        scratch_shapes=[
            pltpu.VMEM(u_factor.shape, BF16),
            pltpu.VMEM(v_factor.shape, BF16),
            pltpu.VMEM((chips, tile_cols, 2 * LANES, tile_size), BF16),
            pltpu.VMEM((chips, tile_cols, 2 * LANES, tile_size), BF16),
            pltpu.VMEM((tile_cols, chips, rows, 2 * LANES), BF16),
            pltpu.VMEM((2, chips, 2, rows, LANES), BF16),
            pltpu.VMEM((2, chips, rows, LANES), BF16),
            pltpu.VMEM((2, chips, rows, LANES), BF16),
            pltpu.VMEM((chips, rows, LANES), F32),
            pltpu.VMEM((2, chips, rows + 16, LANES), BF16),
            pltpu.VMEM((2, chips, rows + 16, LANES), BF16),
            pltpu.VMEM((tile_cols, rows, tile_size), F32),
            pltpu.VMEM((2, nz, *seg), BF16),
            pltpu.VMEM((2, nz, *seg), BF16),
            pltpu.VMEM((2, nz, *seg), BF16),
            pltpu.VMEM((chips * tile_cols, zrows, tile_size), BF16),
            pltpu.VMEM((chips * tile_cols, zrows, tile_size), BF16),
            pltpu.VMEM((2, 2, *seg), BF16),
            pltpu.VMEM((2, *seg), BF16),
            pltpu.VMEM((2, nz, *seg), BF16),
            pltpu.VMEM((4, rows, LANES), F32),
            pltpu.VMEM((2, 1, LANES), F32),
            pltpu.VMEM((2, 1, LANES), F32),
            pltpu.VMEM((1, LANES), F32),
            pltpu.VMEM((chips, 1, LANES), F32),
            pltpu.VMEM((2, 1, LANES), F32),
            pltpu.VMEM((2, nz, 1, LANES), F32),
            pltpu.VMEM((1, LANES), F32),
            pltpu.VMEM((2 * nz, 1, LANES), F32),
            dma((chips,)),
            dma((14,)), dma((13,)),
            dma((chips,)), dma((chips,)), dma((chips,)),
            dma((tile_cols,)), dma((tile_cols,)),
            dma((2,)), dma((2,)),
        ],
        compiler_params=pltpu.CompilerParams(
            collective_id=0, has_side_effects=True, vmem_limit_bytes=60 * 2**20
        ),
        name="lsqr",
    )(rhs.reshape(rows, LANES), u_factor, v_factor, ranks.T, assign)
    last_adjoint(d_hat, v_hats, scalars[1:5, :sources], u_factor, v_factor, ranks)
    out, phibar = pl.pallas_call(
        functools.partial(combine, nz),
        out_shape=[
            jax.ShapeDtypeStruct((rows, tile_cols * tile_size), F32),
            jax.ShapeDtypeStruct((1, sources), F32),
        ],
        in_specs=[vmem] * 2,
        out_specs=[vmem] * 2,
        name="combine",
    )(scalars, natural)
    return out.reshape(2, sources, tile_cols * tile_size), phibar.reshape(sources)


def solution(mesh):
    return jax.shard_map(
        functools.partial(on_device, mesh.shape["row"]),
        mesh=mesh,
        in_specs=(
            P(None, None, "row", "col"),
            P("row", "col", None, None, None),
            P("row", "col", None, None, None),
            P("row", "col"),
            P(),
        ),
        out_specs=(P(None, None, "col"), P()),
        check_vma=False,
    )
```

```python
import functools
import math

import jax
import jax.numpy as jnp
from jax import lax
from jax.experimental import pallas as pl
from jax.experimental.pallas import tpu as pltpu
from jax.sharding import PartitionSpec as P

F32 = jnp.float32
BF16 = jnp.bfloat16
MESH = pl.DeviceIdType.MESH
LANES = 128
GROUP = 2
LOAD = 2
AHEAD = 2
UNROLL = 16
BEHIND = 2


def nn(lhs, rhs):
    return jnp.dot(lhs, rhs, preferred_element_type=F32)


def nt(lhs, rhs):
    return lax.dot_general(lhs, rhs, (((1,), (1,)), ((), ())), preferred_element_type=F32)


def lanes(*parts):
    return jnp.concatenate(parts, axis=1)


def stacked(*parts):
    return jnp.concatenate(parts, axis=0)


def times_factor(vec):
    half = vec.shape[0] // 2
    re, im = vec[:half], vec[half:]
    return stacked(lanes(re, -im), lanes(im, re))


def times_conj_factor(vec):
    half = vec.shape[0] // 2
    re, im = vec[:half], vec[half:]
    return stacked(lanes(re, im), lanes(im, -re))


def to_row(acc):
    pad = jnp.zeros((LANES - acc.shape[0], LANES), F32)
    return jnp.sum(stacked(acc, pad).T, axis=0, keepdims=True)


def to_col(row, sources):
    col = jnp.broadcast_to(row, (LANES, LANES)).T[:sources]
    return stacked(col, col)


def kernel(
    dims,
    rhs,
    u_hbm,
    v_hbm,
    ranks,
    assign,
    nat_out,
    phi_out,
    d_out,
    v_own,
    u_fac,
    v_fac,
    u_tr,
    v_tr,
    coeffs,
    d_full,
    x_send,
    x_recv,
    y_own,
    y_send,
    y_recv,
    z_acc,
    z_send,
    z_recv,
    v_full,
    gathered0,
    gathered1,
    picked,
    sib_recv,
    natural,
    cols,
    pair_send,
    pair_recv,
    row_send,
    row_recv,
    zrow_send,
    zrow_recv,
    last_send,
    last_recv,
    fac_sem,
    send,
    recv,
    ag_r,
    fw_r,
    xs_r,
    zs_r,
    zg_r,
    ng_r,
    sib_r,
):
    chips, nx, ny, nz, tile_cols, sources = dims
    rows = 2 * sources
    zrows = rows // nz
    gathered = (gathered0, gathered1)
    me_c, me_z = lax.axis_index("col"), lax.axis_index("row")
    chip, core = lax.div(me_c, 2), lax.rem(me_c, 2)
    cx, cy = lax.div(chip, ny), lax.rem(chip, ny)
    sibling = chip * 2 + 1 - core

    def hops(q):
        return min(q // ny, nx - q // ny) + min(q % ny, ny - q % ny)

    z_order = sorted(range(1, nz), key=lambda k: -min(k, nz - k))
    near = sorted(range(chips), key=hops)
    far = near[::-1]

    def chip_to(q):
        return lax.rem(cx + lax.div(q, ny), nx) * ny + lax.rem(cy + lax.rem(q, ny), ny)

    def chip_from(q):
        return lax.rem(cx + nx - lax.div(q, ny), nx) * ny + lax.rem(cy + ny - lax.rem(q, ny), ny)

    def along_z(k):
        return lax.rem(me_z + k, nz)

    def remote(src, dst, send, recv, col, row):
        return pltpu.make_async_remote_copy(
            src_ref=src, dst_ref=dst, send_sem=send, recv_sem=recv,
            device_id=(col, row), device_id_type=MESH,
        )

    def copy_ag(rd, q):
        own = d_full.at[rd, chip, core]
        return remote(own, own, send.at[0], ag_r.at[q], chip_to(q) * 2 + core, me_z)

    def copy_fw(rd, q):
        here = d_full.at[rd, chip_from(q), core]
        return remote(here, here, send.at[1], fw_r.at[q], sibling, me_z)

    def copy_xs(rd, q):
        i = chip_to(q)
        return remote(
            x_send.at[rd, i], x_recv.at[rd, i], send.at[2], xs_r.at[q], sibling, me_z
        )

    def copy_ys(rd, q):
        i = chip_to(q)
        return remote(
            y_send.at[rd, i], y_recv.at[rd, q], send.at[3], recv.at[3], i * 2 + core, me_z
        )

    def copy_pair(rd):
        return remote(
            pair_send.at[rd], pair_recv.at[rd], send.at[4], recv.at[4], sibling, me_z
        )

    def copy_row(rd, q):
        return remote(
            row_send.at[rd], row_recv.at[rd, q], send.at[5], recv.at[13 if rd == 2 else 5],
            chip_to(q) * 2 + core, me_z,
        )

    def copy_zrow(rd, k):
        return remote(
            zrow_send.at[rd], zrow_recv.at[rd, k], send.at[6], recv.at[6], me_c, along_z(k)
        )

    def beside(m):
        return chip * 2 + lax.rem(core + m % 2, 2), along_z(m // 2)

    def copy_last(m):
        return remote(last_send, last_recv.at[m], send.at[13], recv.at[12], *beside(m))

    def copy_zs(rd, k, p):
        return remote(
            z_send.at[rd, along_z(k), p], z_recv.at[rd, k, p], send.at[7], zs_r.at[p], me_c,
            along_z(k),
        )

    def copy_zg(rd, k, p):
        own = v_full.at[rd, me_z, p]
        return remote(own, own, send.at[8], zg_r.at[p], me_c, along_z(k))

    def copy_ng(rd, q):
        own = gathered[rd].at[pl.ds(chip * tile_cols, tile_cols)]
        return remote(own, own, send.at[9 + 3 * rd], ng_r.at[rd], chip_to(q) * 2 + core, me_z)

    def copy_sib(rd):
        return remote(
            picked.at[rd, 1 - core], sib_recv.at[rd], send.at[10], sib_r.at[rd], sibling, me_z
        )

    def copy_nz(rd, k):
        own = natural.at[rd, me_z]
        return remote(own, own, send.at[11], recv.at[11], me_c, along_z(k))

    def arrived(ref, sem):
        remote(ref, ref, sem, sem, sibling, me_z).wait_recv()

    def has_left(ref, sem):
        remote(ref, ref, sem, sem, sibling, me_z).wait_send()

    def loop(low, high, body):
        lax.fori_loop(low, high, lambda i, c: (body(i), c)[1], 0)

    def factor_copies(g):
        some = pl.ds(g * LOAD, LOAD)
        return (
            pltpu.make_async_copy(v_hbm.at[some], v_fac.at[some], fac_sem.at[2 * g]),
            pltpu.make_async_copy(u_hbm.at[some], u_fac.at[some], fac_sem.at[2 * g + 1]),
        )

    lane = lax.broadcasted_iota(jnp.int32, (rows, LANES), 1)

    def masked(value, i, p):
        return jnp.where(lane < ranks[p, i], value, 0.0).astype(BF16)

    def lane_sums(square, acc):
        for at in range(0, square.shape[1], LANES):
            part = square[:, at : at + LANES]
            acc = acc + part[:sources] + part[sources:]
        return acc

    def transpose(fac, held, i):
        for p in range(tile_cols):
            for c in range(2):
                held[i, p, c * LANES : (c + 1) * LANES] = fac[i, p, c].T

    barrier = pltpu.get_barrier_semaphore()

    def greet(col, row):
        pl.semaphore_signal(barrier, inc=1, device_id=(col, row), device_id_type=MESH)

    for m in range(1, 2 * nz):
        greet(*beside(m))
    loop(1, chips, lambda q: greet(chip_to(q) * 2 + core, me_z))
    def start_factor(g):
        for copy in factor_copies(g):
            copy.start()

    loop(0, chips // LOAD, start_factor)
    d_full[0, chip, core] = rhs[...].astype(BF16)

    pl.semaphore_wait(barrier, chips - 1 + 2 * nz - 1)

    def send_data(rd):
        copy_fw(rd, 0).start()
        for q in far[:-1]:
            copy_ag(rd, q).start()

    send_data(0)

    def ready(g):
        for copy in factor_copies(g):
            copy.wait()
        for i in range(LOAD):
            transpose(v_fac, v_tr, g * LOAD + i)

    loop(0, chips // LOAD, ready)

    def adjoint(rd):
        def pass_on(q):
            copy_ag(rd, q).wait_recv()
            copy_fw(rd, q).start()

        for q in near[1 : AHEAD * GROUP]:
            pass_on(q)

        acc = jnp.zeros((sources, LANES), F32)
        for g in range(chips // GROUP):
            for q in near[(g + AHEAD) * GROUP : (g + AHEAD + 1) * GROUP]:
                pass_on(q)
            for q in near[g * GROUP : (g + 1) * GROUP]:
                i = chip_from(q)
                copy_fw(rd, q).wait_recv()
                data = lanes(d_full[rd, i, 0], d_full[rd, i, 1])
                wide = data.astype(F32)
                acc = lane_sums(wide * wide, acc)
                left = times_conj_factor(data)
                right = lanes(*[u_fac[i, p].reshape(-1, LANES) for p in range(tile_cols)])
                raw = nn(left, right)
                for p in range(tile_cols):
                    coeff = masked(raw[:, p * LANES : (p + 1) * LANES], i, p)
                    coeffs[p, i] = times_conj_factor(coeff)
            some = [chip_from(q) for q in near[g * GROUP : (g + 1) * GROUP]]
            last = g == chips // GROUP - 1
            if last:
                zrow_start(rd, to_row(acc))
            for p in range(tile_cols):
                left = lanes(*[coeffs[p, i] for i in some])
                z = nn(left, stacked(*[v_tr[i, p] for i in some]))
                if g > 0:
                    z += z_acc[p]
                z_acc[p] = z
                if last:
                    for r in range(nz):
                        z_send[rd, r, p] = z[r * zrows : (r + 1) * zrows].astype(BF16)
                    for k in z_order:
                        copy_zs(rd, k, p).start()

    def zrow_start(rd, row):
        zrow_send[rd] = row
        for k in range(1, nz):
            copy_zrow(rd, k).start()

    def zrow_sum(rd):
        total = zrow_send[rd]
        arrived(zrow_recv.at[rd, pl.ds(1, nz - 1)], recv.at[6])
        for k in range(1, nz):
            total = total + zrow_recv[rd, k]
        return total

    own_rows = pl.ds(pl.multiple_of(me_z * zrows, zrows), zrows)

    def own_col(slot):
        part = cols[slot, own_rows, :]
        return lanes(part, part)

    def model(rd, finish):
        for p in range(tile_cols):
            total = z_acc[p, own_rows, :]
            arrived(z_recv.at[rd, pl.ds(1, nz - 1), p], zs_r.at[p])
            for k in range(1, nz):
                total = total + z_recv[rd, k, p].astype(F32)
            v_hat = finish(total, p)
            v_own[rd, p] = v_hat
            v_b = v_hat.astype(BF16)
            v_full[rd, me_z, p] = v_b
            for k in z_order:
                copy_zg(rd, k, p).start()
            gathered[rd][chip * tile_cols + p] = v_b
        loop(1, chips, lambda q: copy_ng(rd, q).start())

    def forward(rd):
        acc = jnp.zeros((sources, LANES), F32)
        for p in range(tile_cols):
            arrived(v_full.at[rd, pl.ds(0, nz - 1), p], zg_r.at[p])
            vec = stacked(*[v_full[rd, r, p] for r in range(nz)])
            wide = vec.astype(F32)
            acc = lane_sums(wide * wide, acc)
            left = times_factor(vec)

            def group(g, left=left, p=p):
                some = min(UNROLL, chips)
                for h in range(some // 2):
                    where = [g * some + h * 2 + j for j in range(2)]
                    right = lanes(*[v_fac[i, p].reshape(-1, LANES) for i in where])
                    raw = nn(left, right)
                    for j, i in enumerate(where):
                        coeff = masked(raw[:, j * LANES : (j + 1) * LANES], i, p)
                        coeffs[p, i] = times_factor(coeff)

            loop(0, chips // min(UNROLL, chips), group)
        own = to_row(acc)
        pair_send[rd] = own
        copy_pair(rd).start()

        def compute(g):
            for q in far[g * GROUP : (g + 1) * GROUP]:
                i = chip_to(q)
                left = lanes(*[coeffs[p, i] for p in range(tile_cols)])
                y = nn(left, stacked(*[u_tr[i, p] for p in range(tile_cols)]))
                zero, one = y[:, :LANES], y[:, LANES:]
                y_own[i] = jnp.where(core == 0, zero, one)
                x_send[rd, i] = jnp.where(core == 0, one, zero).astype(BF16)
                copy_xs(rd, q).start()

        def finish(g):
            for q in far[g * GROUP : (g + 1) * GROUP]:
                i = chip_to(q)
                copy_xs(rd, q).wait_recv()
                y_send[rd, i] = (y_own[i] + x_recv[rd, i].astype(F32)).astype(BF16)

                if q > 0:
                    copy_ys(rd, q).start()

        behind = min(BEHIND, chips // GROUP)
        for g in range(behind):
            compute(g)
        copy_pair(rd).wait_recv()
        row_send[rd] = own + pair_recv[rd]
        for q in far[:-1]:
            copy_row(rd, q).start()

        for g in range(behind, chips // GROUP):
            compute(g)
            finish(g - behind)
        for g in range(chips // GROUP - behind, chips // GROUP):
            finish(g)

    def data_sum(rd):
        total = y_send[rd, chip].astype(F32)
        arrived(y_recv.at[rd, pl.ds(1, chips - 1)], recv.at[3])
        for q in range(1, chips):
            total = total + y_recv[rd, q].astype(F32)
        return total

    def row_sum(rd):
        total = row_send[rd]
        arrived(row_recv.at[rd, pl.ds(1, chips - 1)], recv.at[13 if rd == 2 else 5])
        for q in range(1, chips):
            total = total + row_recv[rd, q]
        return total

    def pick(rd, held):
        arrived(gathered[rd].at[pl.ds(0, (chips - 1) * tile_cols)], ng_r.at[rd])
        for j, (found, at) in enumerate(held):
            seg = gathered[rd][at].astype(F32) * found.astype(F32)
            picked[rd, j // tile_cols, j % tile_cols] = seg.astype(BF16)
        copy_sib(rd).start()

    def join(rd):
        copy_sib(rd).wait_recv()
        mine = picked[rd, core].astype(F32) + sib_recv[rd].astype(F32)
        natural[rd, me_z] = mine.astype(BF16)
        for k in range(1, nz):
            copy_nz(rd, k).start()

    def find_held():
        first = chip * (2 * tile_cols)
        zero = jnp.int32(0)

        def step(a, carry):
            found, at = list(carry[0]), list(carry[1])
            for t in range(tile_cols):
                held = assign[a * (2 * tile_cols) + core * tile_cols + t] - first
                for j in range(2 * tile_cols):
                    hit = held == j
                    found[j] = jnp.where(hit, 1, found[j])
                    at[j] = jnp.where(hit, a * tile_cols + t, at[j])
            return tuple(found), tuple(at)

        many = 2 * tile_cols
        found, at = lax.fori_loop(0, chips, step, ((zero,) * many, (zero,) * many))
        return list(zip(found, at))

    adjoint(0)
    def transpose_some(g):
        for i in range(4):
            transpose(u_fac, u_tr, g * 4 + i)

    loop(0, chips // 4, transpose_some)
    beta0 = jnp.sqrt(zrow_sum(0))
    cols[0] = to_col(beta0, sources)
    by_beta = own_col(0)
    model(0, lambda total, p: total / by_beta)

    forward(0)
    held = find_held()
    alpha0 = jnp.sqrt(row_sum(0))
    cols[1] = to_col(alpha0, sources)
    y = data_sum(0)
    d_hat = y / cols[1] - cols[1] * (rhs[...] / cols[0])
    d_full[1, chip, core] = d_hat.astype(BF16)
    send_data(1)
    d_out[...] = d_hat
    adjoint(1)
    beta1 = jnp.sqrt(zrow_sum(1))
    cols[2] = to_col(beta1, sources)
    beta, alpha = own_col(2), own_col(1)
    model(1, lambda total, p: total / beta - beta * (v_own[0, p] / alpha))

    pick(0, held)
    forward(1)
    alpha1 = jnp.sqrt(row_sum(1))
    cols[3] = to_col(alpha1, sources)
    y = data_sum(1)
    d_hat = y / cols[3] - cols[3] * (d_out[...] / cols[2])
    square = d_hat * d_hat
    own = to_row(square[:sources] + square[sources:])
    row_send[2] = own
    for q in far[:-1]:
        copy_row(2, q).start()
    join(0)
    pick(1, held)
    d_out[...] = d_hat
    join(1)
    rho1 = jnp.sqrt(alpha0 * alpha0 + beta1 * beta1)
    cosine = alpha0 / rho1
    sine = beta1 / rho1
    theta = sine * alpha1
    rhobar = -cosine * alpha1
    phi1 = cosine * beta0
    phibar = sine * beta0
    total = row_sum(2)
    last_send[...] = total
    for m in range(1, 2 * nz):
        copy_last(m).start()
    arrived(natural.at[:, pl.ds(0, nz - 1)], recv.at[11])
    nat_out[...] = natural[...]
    arrived(last_recv.at[pl.ds(1, 2 * nz - 1)], recv.at[12])
    for m in range(1, 2 * nz):
        total = total + last_recv[m]
    beta2 = jnp.sqrt(total)
    rho2 = jnp.sqrt(rhobar * rhobar + beta2 * beta2)
    cosine = rhobar / rho2
    sine = beta2 / rho2
    step2 = cosine * phibar / rho2
    phi_out[...] = jnp.zeros_like(phi_out)
    phi_out[0:1] = sine * phibar
    phi_out[1:2] = sine / rho2
    phi_out[2:3] = theta / rho1
    phi_out[3:4] = alpha0
    phi_out[4:5] = alpha1
    phi_out[5:6] = (phi1 / rho1 - step2 * (theta / rho1)) / alpha0
    phi_out[6:7] = step2 / alpha1

    others, zs = pl.ds(1, chips - 1), pl.ds(1, nz - 1)
    has_left(d_full.at[:, others, 0], send.at[0])
    has_left(d_full.at[:, :, 0], send.at[1])
    has_left(x_send, send.at[2])
    has_left(y_send.at[:, others], send.at[3])
    has_left(pair_send, send.at[4])
    has_left(row_recv.at[:, others], send.at[5])
    has_left(zrow_recv.at[:, zs], send.at[6])
    has_left(z_send.at[:, zs], send.at[7])
    has_left(v_full.at[:, zs], send.at[8])
    for rd in range(2):
        has_left(gathered[rd].at[pl.ds(0, (chips - 1) * tile_cols)], send.at[9 + 3 * rd])
    has_left(picked.at[0], send.at[10])
    has_left(natural.at[:, zs], send.at[11])
    has_left(last_recv.at[pl.ds(1, 2 * nz - 1)], send.at[13])


def combine(nz, scalars, natural, out, phi):
    sources = phi.shape[1]
    _, _, tile_cols, _, width = natural.shape
    first, second = to_col(scalars[5:6], sources), to_col(scalars[6:7], sources)
    phi[...] = scalars[0:1, :sources]
    for p in range(tile_cols):
        for at in range(0, width, LANES):
            one = stacked(*[natural[0, r, p, :, at : at + LANES] for r in range(nz)])
            two = stacked(*[natural[1, r, p, :, at : at + LANES] for r in range(nz)])
            out[:, p * width + at : p * width + at + LANES] = (
                first * one.astype(F32) + second * two.astype(F32)
            )


def last_adjoint(d_hat, v_hats, scalars, u_factor, v_factor, ranks):
    tile_rows, tile_cols, _, tile_size, rank_cap = u_factor.shape
    sources = d_hat.shape[0] // 2
    rank_iota = lax.broadcasted_iota(jnp.int32, (tile_rows, tile_cols, 1, 1, rank_cap), 4)
    mask = (rank_iota < ranks[:, :, None, None, None]).astype(F32)
    d_hat = d_hat.reshape(2, sources, -1)
    beta = jnp.sqrt(lax.psum(jnp.sum(d_hat * d_hat, axis=(0, 2)), ("col", "row")))
    data = lax.all_gather(d_hat.astype(BF16), "col", axis=2, tiled=True)
    data = data.reshape(2, sources, tile_rows, tile_size)
    raw = jnp.einsum("ipcnk,dsin->ipcdsk", u_factor, data, preferred_element_type=F32)
    coeff = jnp.stack([raw[:, :, 0, 0] + raw[:, :, 1, 1], raw[:, :, 0, 1] - raw[:, :, 1, 0]], axis=2)
    coeff = (coeff * mask).astype(BF16)
    prod = jnp.einsum("ipcnk,ipdsk->cdspn", v_factor, coeff, preferred_element_type=F32)
    model = jnp.stack([prod[0, 0] + prod[1, 1], prod[0, 1] - prod[1, 0]], axis=0)
    model = lax.psum(model, "row").reshape(2, sources, tile_cols * tile_size)
    sine_by_rho, theta_by_rho, alpha0, alpha1 = [row[None, :, None] for row in scalars]
    v_hats = lax.all_gather(v_hats, "row", axis=2, tiled=True)
    v_hats = v_hats.transpose(0, 2, 1, 3).reshape(2, *model.shape)
    v_prev = v_hats[1] / alpha1
    w_prev = v_prev - theta_by_rho * (v_hats[0] / alpha0)
    v_hat = model / beta[None, :, None] - beta[None, :, None] * v_prev
    alpha = jnp.sqrt(lax.psum(jnp.sum(v_hat * v_hat, axis=(0, 2)), "col"))
    v_vec = v_hat / alpha[None, :, None]
    return v_vec, alpha, v_vec - sine_by_rho * alpha[None, :, None] * w_prev


def on_device(nz, rhs, u_factor, v_factor, ranks, assign):
    tile_rows, tile_cols, _, tile_size, _ = u_factor.shape
    sources = rhs.shape[1]
    rows = 2 * sources
    zrows = rows // nz
    chips = tile_rows
    ny = math.isqrt(chips)
    nx = chips // ny
    dims = (chips, nx, ny, nz, tile_cols, sources)
    seg = (tile_cols, zrows, tile_size)
    dma = pltpu.SemaphoreType.DMA
    vmem = pl.BlockSpec(memory_space=pltpu.VMEM)
    smem = pl.BlockSpec(memory_space=pltpu.SMEM)
    hbm = pl.BlockSpec(memory_space=pl.ANY)
    natural, scalars, d_hat, v_hats = pl.pallas_call(
        functools.partial(kernel, dims),
        out_shape=[
            jax.ShapeDtypeStruct((2, nz, *seg), BF16),
            jax.ShapeDtypeStruct((8, LANES), F32),
            jax.ShapeDtypeStruct((rows, LANES), F32),
            jax.ShapeDtypeStruct((2, *seg), F32),
        ],
        in_specs=[vmem, hbm, hbm, smem, smem],
        out_specs=[vmem] * 4,
        scratch_shapes=[
            pltpu.VMEM(u_factor.shape, BF16),
            pltpu.VMEM(v_factor.shape, BF16),
            pltpu.VMEM((chips, tile_cols, 2 * LANES, tile_size), BF16),
            pltpu.VMEM((chips, tile_cols, 2 * LANES, tile_size), BF16),
            pltpu.VMEM((tile_cols, chips, rows, 2 * LANES), BF16),
            pltpu.VMEM((2, chips, 2, rows, LANES), BF16),
            pltpu.VMEM((2, chips, rows, LANES), BF16),
            pltpu.VMEM((2, chips, rows, LANES), BF16),
            pltpu.VMEM((chips, rows, LANES), F32),
            pltpu.VMEM((2, chips, rows, LANES), BF16),
            pltpu.VMEM((2, chips, rows, LANES), BF16),
            pltpu.VMEM((tile_cols, rows, tile_size), F32),
            pltpu.VMEM((2, nz, *seg), BF16),
            pltpu.VMEM((2, nz, *seg), BF16),
            pltpu.VMEM((2, nz, *seg), BF16),
            pltpu.VMEM((chips * tile_cols, zrows, tile_size), BF16),
            pltpu.VMEM((chips * tile_cols, zrows, tile_size), BF16),
            pltpu.VMEM((2, 2, *seg), BF16),
            pltpu.VMEM((2, *seg), BF16),
            pltpu.VMEM((2, nz, *seg), BF16),
            pltpu.VMEM((4, rows, LANES), F32),
            pltpu.VMEM((2, 1, LANES), F32),
            pltpu.VMEM((2, 1, LANES), F32),
            pltpu.VMEM((3, 1, LANES), F32),
            pltpu.VMEM((3, chips, 1, LANES), F32),
            pltpu.VMEM((2, 1, LANES), F32),
            pltpu.VMEM((2, nz, 1, LANES), F32),
            pltpu.VMEM((1, LANES), F32),
            pltpu.VMEM((2 * nz, 1, LANES), F32),
            dma((chips,)),
            dma((14,)), dma((14,)),
            dma((chips,)), dma((chips,)), dma((chips,)),
            dma((tile_cols,)), dma((tile_cols,)),
            dma((2,)), dma((2,)),
        ],
        compiler_params=pltpu.CompilerParams(
            collective_id=0, has_side_effects=True, vmem_limit_bytes=60 * 2**20
        ),
        name="lsqr",
    )(rhs.reshape(rows, LANES), u_factor, v_factor, ranks.T, assign)
    last_adjoint(d_hat, v_hats, scalars[1:5, :sources], u_factor, v_factor, ranks)
    out, phibar = pl.pallas_call(
        functools.partial(combine, nz),
        out_shape=[
            jax.ShapeDtypeStruct((rows, tile_cols * tile_size), F32),
            jax.ShapeDtypeStruct((1, sources), F32),
        ],
        in_specs=[vmem] * 2,
        out_specs=[vmem] * 2,
        name="combine",
    )(scalars, natural)
    return out.reshape(2, sources, tile_cols * tile_size), phibar.reshape(sources)


def solution(mesh):
    return jax.shard_map(
        functools.partial(on_device, mesh.shape["row"]),
        mesh=mesh,
        in_specs=(
            P(None, None, "row", "col"),
            P("row", "col", None, None, None),
            P("row", "col", None, None, None),
            P("row", "col"),
            P(),
        ),
        out_specs=(P(None, None, "col"), P()),
        check_vma=False,
    )
```
